32 devices in a mesh: dp: 8 (over z, core), sub: 4 (over y, x).
Axes of the slice: x: 2, y: 2, z: 4, core: 2. Of those that a mesh axis runs over, the one named last changes fastest.
Arguments:
- samples: bfloat16 [4096, 256], P(('dp', 'sub')), may hold values from -12 to 12
- rotation: bfloat16 [256, 256], P(None, 'sub'), may hold values from -0.375 to 0.375
- codebook: float32 [4, 256, 64], P('sub'), may hold values from -4 to 4
Outputs:
- recon: bfloat16 [4096, 256], P(('dp', 'sub'))
- new_codebook: float32 [4, 256, 64], P('sub')
- cross: float32 [256, 256], P(('dp', 'sub'))
The draws below stay inside these ranges and needn't reach their ends.
All inputs are finite; a program needn't handle non-finite values.
Results may differ from the reference program's by a relative error of at most 0.02.
Values may be sent and summed in bfloat16 or wider, within the bound.
A program may use at most 64 MiB of HBM per device.

```python
import jax
import jax.numpy as jnp

SUB_DIM = 64
CODES = 256
ROWS_DEV = 128
SUBS = 4
DIM = 256
ROWS = 4096


def draw_samples(key, part):
    key = jax.random.fold_in(key, 7)
    first = jax.random.fold_in(key, 0)
    fourth = jax.random.fold_in(key, 3)
    values = jax.random.normal(first, (ROWS, DIM), jnp.float32)
    blocks = ROWS // ROWS_DEV
    width = DIM // blocks
    pairing = jax.random.permutation(fourth, blocks)
    row_block = jnp.arange(ROWS) // ROWS_DEV
    column_block = jnp.arange(DIM) // width
    heavy = pairing[row_block][:, None] == column_block[None, :]
    values = jnp.where(heavy, 6.0 * values, values)
    return jnp.clip(values, -12.0, 12.0).astype(jnp.bfloat16)


def block_levels(key, shape, shards, low, largest):
    gain, own = 1.0, jax.random.fold_in(key, 6)
    for dim, shards_of in shards:
        draws = jnp.exp(jax.random.uniform(jax.random.fold_in(own, dim), (shards_of,), jnp.float32, low / len(shards), largest / len(shards)))
        gain = gain * jnp.repeat(draws, shape[dim] // shards_of).reshape([-1 if axis == dim else 1 for axis in range(len(shape))])
    return gain


def centred(stream_key, shape, scale, most, shards=(), kind=jnp.bfloat16):
    values = jax.random.normal(stream_key, shape, jnp.float32) * scale
    if len(shards) > 0:
        values = block_levels(stream_key, shape, shards, -0.22, 0.18) * values
    return jnp.clip(values, min=-most, max=most).astype(kind)


def setup_inputs(seed: int = 0) -> dict:
    key_list = jax.random.split(jax.random.key(seed), 4)
    samples = draw_samples(jax.random.fold_in(key_list[3], 71), 0)
    rotation = centred(key_list[1], (DIM, DIM), DIM ** -0.5, 0.375, ((1, 4),))
    codebook = centred(key_list[2], (SUBS, CODES, SUB_DIM), 1.0, 4.0, ((0, 4),), jnp.float32)
    return {"samples": samples, "rotation": rotation, "codebook": codebook}


def reference(samples, rotation, codebook):
    total_rows = samples.shape[0]
    block_rows = min(8192, total_rows)
    count_blocks = total_rows // block_rows
    codes_low = codebook.astype(jnp.bfloat16).astype(jnp.float32)
    code_square = jnp.sum(codebook * codebook, axis=-1)

    def step(carry, sample_block):
        sums, counts, cross = carry
        rotated = jnp.dot(sample_block, rotation, preferred_element_type=jnp.float32).astype(jnp.bfloat16)
        parts = rotated.reshape(block_rows, SUBS, SUB_DIM).astype(jnp.float32)
        inner = jnp.einsum('bsk,sck->bsc', parts, codes_low)
        row_square = jnp.sum(parts * parts, axis=-1)[..., None]
        logits = -0.125 * (row_square - 2.0 * inner + code_square[None])
        weights = jax.nn.softmax(logits, axis=-1).astype(jnp.bfloat16).astype(jnp.float32)
        rebuilt = jnp.einsum('bsc,sck->bsk', weights, codes_low).astype(jnp.bfloat16).reshape(block_rows, DIM)
        sums = sums + jnp.einsum('bsc,bsk->sck', weights, parts)
        counts = counts + jnp.sum(weights, axis=0)
        cross = cross + jnp.dot(sample_block.T, rebuilt, preferred_element_type=jnp.float32)
        return (sums, counts, cross), rebuilt

    start = (jnp.zeros((SUBS, CODES, SUB_DIM), jnp.float32), jnp.zeros((SUBS, CODES), jnp.float32), jnp.zeros((DIM, DIM), jnp.float32))
    (sums, counts, cross), rebuilt = jax.lax.scan(step, start, samples.reshape(count_blocks, block_rows, DIM))
    new_codebook = (sums + codebook) / (counts[..., None] + 1.0)
    return rebuilt.reshape(total_rows, DIM), new_codebook, cross
```

```python
import functools

import jax
import jax.numpy as jnp
from jax import lax
from jax.experimental import pallas as pl
from jax.experimental.pallas import tpu as pltpu
from jax.sharding import PartitionSpec as P

MESH = pl.DeviceIdType.MESH
F32 = jnp.float32
BF16 = jnp.bfloat16
LANES = 128
NT = (((1,), (1,)), ((), ()))
TN = (((0,), (0,)), ((), ()))


def each(count, body, start=0):
    if count - start <= 16:
        for i in range(start, count):
            body(i)
    else:
        def step(i, carry):
            body(i)
            return carry

        lax.fori_loop(start, count, step, 0)


def kernel(
    dp,
    subs,
    samples_ref,
    rotation_ref,
    codebook_ref,
    recon_ref,
    new_ref,
    cross_ref,
    rot_all,
    code_all,
    rec_all,
    pack_s,
    pack_x,
    one_s,
    one_x,
    comb_s,
    comb_x,
    two_s,
    two_x,
    rot_send,
    rot_recv,
    code_send,
    code_recv,
    one_send,
    one_recv,
    two_s_send,
    two_s_recv,
    two_x_send,
    two_x_recv,
    new_send,
    new_recv,
):
    half = dp // 2
    group = half * subs
    my_dp = lax.axis_index("dp")
    my_sub = lax.axis_index("sub")
    core = lax.rem(my_dp, 2)
    pair = my_dp // 2
    me = pair * subs + my_sub
    rows, dim = samples_ref.shape
    codes, width = codebook_ref.shape[1:]
    chunk = codes // dp
    out_rows = cross_ref.shape[0]

    barrier = pltpu.get_barrier_semaphore()

    def same_core(k):
        n = lax.rem(me + k, group)
        return (2 * (n // subs) + core, lax.rem(n, subs))

    def greet(k):
        pl.semaphore_signal(barrier, inc=1, device_id=same_core(k), device_id_type=MESH)

    def greet_other(k):
        p = lax.rem(pair + k, half)
        pl.semaphore_signal(
            barrier, inc=1, device_id=(2 * p + 1 - core, my_sub), device_id_type=MESH
        )

    each(group, greet, 1)
    each(half, greet_other)

    rot_all[my_sub] = rotation_ref[...].astype(F32).T.astype(BF16)
    code_t = codebook_ref[0].T
    square = jnp.sum(code_t * code_t, axis=0, keepdims=True)
    high = square.astype(BF16).astype(F32)
    middle = (square - high).astype(BF16).astype(F32)
    low = square - high - middle
    row = lax.broadcasted_iota(jnp.int32, (16, codes), 0)
    split = jnp.where(row == 0, high, jnp.where(row == 1, middle, jnp.where(row == 2, low, 0.0)))
    code_all[my_sub, 0:width] = code_t.astype(BF16)
    code_all[my_sub, width : width + 16] = split.astype(BF16)

    pl.semaphore_wait(barrier, group - 1 + half)

    def gather_copy(buffer, send, recv, k, index):
        return pltpu.make_async_remote_copy(
            src_ref=buffer.at[index],
            dst_ref=buffer.at[index],
            send_sem=send.at[k - 1],
            recv_sem=recv.at[k - 1],
            device_id=(my_dp, lax.rem(my_sub + k, subs)),
            device_id_type=MESH,
        )

    def send_gather(k):
        gather_copy(rot_all, rot_send, rot_recv, k, my_sub).start()
        gather_copy(code_all, code_send, code_recv, k, my_sub).start()

    each(subs, send_gather, 1)

    samples = samples_ref[...]
    ones = jnp.ones((rows, LANES - width), BF16)

    def assign(k):
        s = lax.rem(my_sub + subs - k, subs)
        if k > 0:
            gather_copy(rot_all, rot_send, rot_recv, k, s).wait_recv()
            gather_copy(code_all, code_send, code_recv, k, s).wait_recv()
        rotated = lax.dot_general(samples, rot_all[s], NT, preferred_element_type=F32).astype(BF16)
        wide = rotated.astype(F32)
        row_square = jnp.sum(wide * wide, axis=1, keepdims=True)
        code_low = code_all[s, 0:width]
        code_square = jnp.sum(code_all[s, width : width + 16].astype(F32), axis=0, keepdims=True)
        inner = jnp.dot(rotated, code_low, preferred_element_type=F32)
        logits = -0.125 * (row_square - 2.0 * inner + code_square)
        powers = jnp.exp(logits - jnp.max(logits, axis=1, keepdims=True))
        weights = (powers / jnp.sum(powers, axis=1, keepdims=True)).astype(BF16)
        rec_all[s] = lax.dot_general(weights, code_low, NT, preferred_element_type=F32).astype(BF16)
        sums = lax.dot_general(
            weights,
            jnp.concatenate([rotated, ones], axis=1),
            TN,
            preferred_element_type=F32,
        ).reshape(half, 2, chunk, LANES)
        if chunk < 16:
            sums = jnp.concatenate(
                [sums, jnp.zeros((half, 2, 16 - chunk, LANES), F32)], axis=2
            )
        sums = sums.astype(BF16)
        for c in range(2):
            pack_s[c, :, s] = sums[:, c]

    for k in range(subs):
        assign(k)

    def swap(pack, one, k):
        return pltpu.make_async_remote_copy(
            src_ref=pack.at[1 - core],
            dst_ref=one,
            send_sem=one_send.at[k],
            recv_sem=one_recv.at[k],
            device_id=(2 * pair + 1 - core, my_sub),
            device_id_type=MESH,
        )

    swap_s = swap(pack_s, one_s, 0)
    swap_s.start()
    recon = jnp.concatenate([rec_all[s] for s in range(subs)], axis=1)
    recon_ref[...] = recon
    cross = lax.dot_general(samples, recon, TN, preferred_element_type=F32)
    cross = cross.reshape(half, 2, subs, out_rows, dim)
    cross = jnp.concatenate(
        [cross[..., j : j + LANES] for j in range(0, dim, LANES)], axis=3
    ).astype(BF16)
    for c in range(2):
        pack_x[c] = cross[:, c]
    swap_x = swap(pack_x, one_x, 1)
    swap_x.start()

    def spread(comb, two, send, recv, k):
        return pltpu.make_async_remote_copy(
            src_ref=comb.at[lax.rem(me + k, group)],
            dst_ref=two.at[k - 1],
            send_sem=send.at[k - 1],
            recv_sem=recv.at[k - 1],
            device_id=same_core(k),
            device_id_type=MESH,
        )

    def spread_s(k):
        return spread(comb_s, two_s, two_s_send, two_s_recv, k)

    def spread_x(k):
        return spread(comb_x, two_x, two_x_send, two_x_recv, k)

    swap_s.wait_recv()
    comb_s[...] = (pack_s[core].astype(F32) + one_s[...].astype(F32)).astype(BF16).reshape(comb_s.shape)
    each(group, lambda k: spread_s(k).start(), 1)
    swap_x.wait_recv()
    comb_x[...] = (pack_x[core].astype(F32) + one_x[...].astype(F32)).astype(BF16).reshape(comb_x.shape)
    each(group, lambda k: spread_x(k).start(), 1)

    each(group, lambda k: spread_s(k).wait_recv(), 1)
    total = comb_s[me].astype(F32) + jnp.sum(two_s[...].astype(F32), axis=0)
    mine = pl.ds(pl.multiple_of(my_dp * chunk, chunk), chunk)
    new_ref[0, mine] = (total[:chunk, :width] + codebook_ref[0, mine]) / (
        total[:chunk, width : 2 * width] + 1.0
    )

    def share(k):
        return pltpu.make_async_remote_copy(
            src_ref=new_ref.at[0, mine],
            dst_ref=new_ref.at[0, mine],
            send_sem=new_send.at[k - 1],
            recv_sem=new_recv.at[k - 1],
            device_id=(lax.rem(my_dp + k, dp), my_sub),
            device_id_type=MESH,
        )

    each(dp, lambda k: share(k).start(), 1)

    each(group, lambda k: spread_x(k).wait_recv(), 1)
    total_x = comb_x[me].astype(F32) + jnp.sum(two_x[...].astype(F32), axis=0)
    for j in range(dim // LANES):
        cross_ref[:, j * LANES : (j + 1) * LANES] = total_x[j * out_rows : (j + 1) * out_rows]

    def finish_gather(k):
        gather_copy(rot_all, rot_send, rot_recv, k, my_sub).wait_send()
        gather_copy(code_all, code_send, code_recv, k, my_sub).wait_send()

    each(subs, finish_gather, 1)
    swap_s.wait_send()
    swap_x.wait_send()
    each(group, lambda k: spread_s(k).wait_send(), 1)
    each(group, lambda k: spread_x(k).wait_send(), 1)
    each(dp, lambda k: share(k).wait_send(), 1)
    each(dp, lambda k: share(k).wait_recv(), 1)


def per_device(dp, subs, samples, rotation, codebook):
    rows, dim = samples.shape
    codes, width = codebook.shape[1:]
    half = dp // 2
    group = half * subs
    chunk = max(16, codes // dp)
    out_rows = dim // (dp * subs)
    tile = out_rows * dim // LANES
    dma = pltpu.SemaphoreType.DMA
    vmem = pl.BlockSpec(memory_space=pltpu.VMEM)
    return pl.pallas_call(
        functools.partial(kernel, dp, subs),
        out_shape=(
            jax.ShapeDtypeStruct((rows, dim), BF16),
            jax.ShapeDtypeStruct((1, codes, width), F32),
            jax.ShapeDtypeStruct((out_rows, dim), F32),
        ),
        in_specs=[vmem] * 3,
        out_specs=(vmem,) * 3,
        scratch_shapes=[
            pltpu.VMEM((subs, width, dim), BF16),
            pltpu.VMEM((subs, width + 16, codes), BF16),
            pltpu.VMEM((subs, rows, width), BF16),
            pltpu.VMEM((2, half, subs, chunk, LANES), BF16),
            pltpu.VMEM((2, half, subs, tile, LANES), BF16),
            pltpu.VMEM((half, subs, chunk, LANES), BF16),
            pltpu.VMEM((half, subs, tile, LANES), BF16),
            pltpu.VMEM((group, chunk, LANES), BF16),
            pltpu.VMEM((group, tile, LANES), BF16),
            pltpu.VMEM((group - 1, chunk, LANES), BF16),
            pltpu.VMEM((group - 1, tile, LANES), BF16),
            dma((subs - 1,)),
            dma((subs - 1,)),
            dma((subs - 1,)),
            dma((subs - 1,)),
            dma((2,)),
            dma((2,)),
            dma((group - 1,)),
            dma((group - 1,)),
            dma((group - 1,)),
            dma((group - 1,)),
            dma((dp - 1,)),
            dma((dp - 1,)),
        ],
        compiler_params=pltpu.CompilerParams(
            collective_id=0, has_side_effects=True, vmem_limit_bytes=48 * 1024 * 1024
        ),
    )(samples, rotation, codebook)


def solution(mesh):
    in_specs = (P(("dp", "sub"), None), P(None, "sub"), P("sub", None, None))
    out_specs = (P(("dp", "sub"), None), P("sub", None, None), P(("dp", "sub"), None))
    return jax.shard_map(
        functools.partial(per_device, mesh.shape["dp"], mesh.shape["sub"]),
        mesh=mesh,
        in_specs=in_specs,
        out_specs=out_specs,
        check_vma=False,
    )
```

```python
import functools

import jax
import jax.numpy as jnp
from jax import lax
from jax.experimental import pallas as pl
from jax.experimental.pallas import tpu as pltpu
from jax.sharding import PartitionSpec as P

MESH = pl.DeviceIdType.MESH
F32 = jnp.float32
BF16 = jnp.bfloat16
LANES = 128
NT = (((1,), (1,)), ((), ()))
TN = (((0,), (0,)), ((), ()))


def each(count, body, start=0):
    if count - start <= 32:
        for i in range(start, count):
            body(i)
    else:
        def step(i, carry):
            body(i)
            return carry

        lax.fori_loop(start, count, step, 0)


def kernel(
    dp,
    subs,
    samples_hbm,
    rotation_hbm,
    codebook_hbm,
    recon_ref,
    new_ref,
    cross_ref,
    samples_all,
    code_own,
    rot_all,
    code_all,
    rec_part,
    rec_halves,
    pack_s,
    pack_x,
    two_s,
    two_x,
    spare,
    halves,
    final,
    local_sem,
    rot_send,
    rot_recv,
    code_send,
    code_recv,
    swap_send,
    swap_recv,
    two_s_send,
    two_s_recv,
    two_x_send,
    two_x_recv,
    new_send,
    new_recv,
):
    chips_z = dp // 2
    half = subs // 2
    group = chips_z * subs
    my_dp = lax.axis_index("dp")
    my_sub = lax.axis_index("sub")
    core = lax.rem(my_dp, 2)
    my_z = my_dp // 2
    me = my_z * subs + my_sub
    _, rows, dim = samples_all.shape
    width, codes = code_own.shape
    chunk = codes // dp
    out_rows = cross_ref.shape[0]
    home = my_sub // half == core
    home_index = lax.rem(my_sub, half)

    load_samples = pltpu.make_async_copy(samples_hbm, samples_all.at[core], local_sem.at[0])
    load_codes = pltpu.make_async_copy(codebook_hbm.at[0], code_own, local_sem.at[1])
    load_rotation = pltpu.make_async_copy(rotation_hbm, rot_all.at[home_index], local_sem.at[2])
    load_codes.start()
    load_samples.start()

    @pl.when(home)
    def _():
        load_rotation.start()

    barrier = pltpu.get_barrier_semaphore()
    everyone = dp * subs
    my_id = my_dp * subs + my_sub

    def greet(k):
        n = lax.rem(my_id + k, everyone)
        pl.semaphore_signal(
            barrier, inc=1, device_id=(n // subs, lax.rem(n, subs)), device_id_type=MESH
        )

    each(everyone, greet, 1)

    load_codes.wait()

    @pl.when(home)
    def _():
        code_t = code_own[...]
        square = jnp.sum(code_t * code_t, axis=0, keepdims=True)
        high = square.astype(BF16).astype(F32)
        middle = (square - high).astype(BF16).astype(F32)
        low = square - high - middle
        row = lax.broadcasted_iota(jnp.int32, (16, codes), 0)
        split = jnp.where(
            row == 0, high, jnp.where(row == 1, middle, jnp.where(row == 2, low, 0.0))
        )
        code_all[home_index, 0:width] = code_t.astype(BF16)
        code_all[home_index, width : width + 16] = split.astype(BF16)
        load_rotation.wait()

    load_samples.wait()
    pl.semaphore_wait(barrier, everyone - 1)

    def swap(src, dst, k):
        return pltpu.make_async_remote_copy(
            src_ref=src,
            dst_ref=dst,
            send_sem=swap_send.at[k],
            recv_sem=swap_recv.at[k],
            device_id=(2 * my_z + 1 - core, my_sub),
            device_id_type=MESH,
        )

    def gather_copy(buffer, send, recv, k, index):
        return pltpu.make_async_remote_copy(
            src_ref=buffer.at[index],
            dst_ref=buffer.at[index],
            send_sem=send.at[k],
            recv_sem=recv.at[index],
            device_id=(my_dp, lax.rem(my_sub + k, subs)),
            device_id_type=MESH,
        )

    @pl.when(home)
    def _():
        def send_gather(k):
            gather_copy(rot_all, rot_send, rot_recv, k, home_index).start()
            gather_copy(code_all, code_send, code_recv, k, home_index).start()

        each(subs, send_gather, 1)

    swap_samples = swap(samples_all.at[core], samples_all.at[core], 0)
    swap_samples.start()
    swap_samples.wait_recv()

    samples = samples_all[...].reshape(2 * rows, dim)
    ones = jnp.ones((2 * rows, LANES - width), BF16)

    def spread(src, two, send, recv, n):
        return pltpu.make_async_remote_copy(
            src_ref=src,
            dst_ref=two.at[me],
            send_sem=send.at[n],
            recv_sem=recv.at[me],
            device_id=(2 * (n // subs) + core, lax.rem(n, subs)),
            device_id_type=MESH,
        )

    def arrived(two, send, recv, n):
        return pltpu.make_async_remote_copy(
            src_ref=two.at[n],
            dst_ref=two.at[n],
            send_sem=send.at[n],
            recv_sem=recv.at[n],
            device_id=(2 * (n // subs) + core, lax.rem(n, subs)),
            device_id_type=MESH,
        )

    def chunk_of(n):
        return lax.rem(n, subs) // half * chips_z + n // subs

    def spread_s(n):
        return spread(pack_s.at[lax.rem(n, half), chunk_of(n)], two_s, two_s_send, two_s_recv, n)

    def assign(i):
        @pl.when(jnp.logical_not(jnp.logical_and(home, home_index == i)))
        def _():
            gather_copy(rot_all, rot_send, rot_recv, 1, i).wait_recv()
            gather_copy(code_all, code_send, code_recv, 1, i).wait_recv()

        rotated = lax.dot_general(samples, rot_all[i], NT, preferred_element_type=F32).astype(BF16)
        wide = rotated.astype(F32)
        row_square = jnp.sum(wide * wide, axis=1, keepdims=True)
        code_low = code_all[i, 0:width]
        code_square = jnp.sum(code_all[i, width : width + 16].astype(F32), axis=0, keepdims=True)
        inner = jnp.dot(rotated, code_low, preferred_element_type=F32)
        logits = -0.125 * (row_square - 2.0 * inner + code_square)
        powers = jnp.exp(logits - jnp.max(logits, axis=1, keepdims=True))
        weights = (powers / jnp.sum(powers, axis=1, keepdims=True)).astype(BF16)
        sums = lax.dot_general(
            weights,
            jnp.concatenate([rotated, ones], axis=1),
            TN,
            preferred_element_type=F32,
        ).reshape(dp, chunk, LANES)
        if chunk < 16:
            sums = jnp.concatenate([sums, jnp.zeros((dp, 16 - chunk, LANES), F32)], axis=1)
        pack_s[i] = sums.astype(BF16)

        def send_sums(m):
            n = half * lax.rem(me // half + m, group // half) + i
            if isinstance(m, int) and m > 0:
                spread_s(n).start()
            else:
                pl.when(n != me)(lambda: spread_s(n).start())

        each(group // half, send_sums)
        return lax.dot_general(weights, code_low, NT, preferred_element_type=F32).astype(BF16)

    recon = jnp.concatenate([assign(i) for i in range(half)], axis=1)
    rec_part[...] = recon.reshape(rec_part.shape)
    swap_recon = swap(rec_part.at[1 - core], rec_halves.at[core], 1)
    swap_recon.start()

    cross = lax.dot_general(samples, recon, TN, preferred_element_type=F32)
    cross = cross.reshape(chips_z, 2, subs, out_rows, dim // 2)
    pack_x[...] = (
        jnp.concatenate(
            [cross[:, c, ..., j : j + LANES] for c in range(2) for j in range(0, dim // 2, LANES)],
            axis=2,
        )
        .astype(BF16)
        .reshape(pack_x.shape)
    )

    def spread_x(k):
        n = lax.rem(me + k, group)
        return spread(pack_x.at[n], two_x, two_x_send, two_x_recv, n)

    each(group, lambda k: spread_x(k).start(), 1)
    rec_halves[core] = rec_part[core]
    two_s[me] = pack_s[lax.rem(me, half), chunk_of(me)]
    two_x[me] = pack_x[me]

    def wait_s(k):
        arrived(two_s, two_s_send, two_s_recv, lax.rem(me + k, group)).wait_recv()

    each(group, wait_s, 1)
    mine = chunk_of(me)
    final[mine] = jnp.sum(two_s[...].astype(F32), axis=0).astype(BF16)
    owned = core * half + home_index

    def share(t):
        return pltpu.make_async_remote_copy(
            src_ref=final.at[mine],
            dst_ref=spare.at[mine],
            send_sem=new_send.at[t],
            recv_sem=new_recv.at[mine],
            device_id=(lax.rem(my_dp + t, dp), owned),
            device_id_type=MESH,
        )

    each(dp, lambda t: share(t).start(), 1)

    @pl.when(home)
    def _():
        spare[mine] = final[mine]

    @pl.when(jnp.logical_not(home))
    def _():
        share(0).start()

    def wait_x(k):
        arrived(two_x, two_x_send, two_x_recv, lax.rem(me + k, group)).wait_recv()

    each(group, wait_x, 1)
    total_x = jnp.sum(two_x[...].astype(F32), axis=0)
    tall = total_x.shape[0] // 2
    final_x = total_x.reshape(2, tall, LANES)
    halves[2:4] = final_x
    swap_x = swap(halves.at[3 - core], halves.at[core], 2)
    swap_x.start()
    halves[core] = halves[2 + core]
    swap_recon.wait_recv()
    for c in range(2):
        recon_ref[:, c * (dim // 2) : (c + 1) * (dim // 2)] = rec_halves[c]

    def received(t):
        j = lax.rem(mine + t, dp)
        return pltpu.make_async_remote_copy(
            src_ref=spare.at[j],
            dst_ref=spare.at[j],
            send_sem=new_send.at[0],
            recv_sem=new_recv.at[j],
            device_id=(my_dp, owned),
            device_id_type=MESH,
        )

    swap_x.wait_recv()
    for c in range(2):
        for j in range(dim // 2 // LANES):
            at = c * (dim // 2) + j * LANES
            cross_ref[:, at : at + LANES] = halves[c, j * out_rows : (j + 1) * out_rows]

    each(dp, lambda t: received(t).wait_recv(), 1)

    @pl.when(jnp.logical_not(home))
    def _():
        received(0).wait_recv()

    totals = spare[...].astype(F32)[:, :chunk].reshape(codes, LANES).T
    new_ref[0] = (totals[:width] + code_own[...]) / (totals[width : 2 * width] + 1.0)

    @pl.when(home)
    def _():
        def finish(k):
            gather_copy(rot_all, rot_send, rot_recv, k, home_index).wait_send()
            gather_copy(code_all, code_send, code_recv, k, home_index).wait_send()

        each(subs, finish, 1)

    @pl.when(jnp.logical_not(home))
    def _():
        share(0).wait_send()

    swap_samples.wait_send()
    swap_recon.wait_send()
    swap_x.wait_send()
    each(group, lambda k: spread_s(lax.rem(me + k, group)).wait_send(), 1)
    each(group, lambda k: spread_x(k).wait_send(), 1)
    each(dp, lambda t: share(t).wait_send(), 1)


def write_kernel(recon_ref, new_ref, cross_ref, recon_out, new_out, cross_out, sems):
    pairs = ((recon_ref, recon_out), (new_ref, new_out), (cross_ref, cross_out))
    copies = [pltpu.make_async_copy(s, d, sems.at[i]) for i, (s, d) in enumerate(pairs)]
    for copy in copies:
        copy.start()
    for copy in copies:
        copy.wait()


def per_device(dp, subs, samples, rotation, codebook):
    rows, dim = samples.shape
    codes, width = codebook.shape[1:]
    half = subs // 2
    group = dp // 2 * subs
    chunk = max(16, codes // dp)
    out_rows = dim // (dp * subs)
    tile = out_rows * dim // LANES
    dma = pltpu.SemaphoreType.DMA
    vmem = pl.BlockSpec(memory_space=pltpu.VMEM)
    hbm = pl.BlockSpec(memory_space=pltpu.HBM)
    shapes = (
        jax.ShapeDtypeStruct((rows, dim), BF16),
        jax.ShapeDtypeStruct((1, width, codes), F32),
        jax.ShapeDtypeStruct((out_rows, dim), F32),
    )
    parts = pl.pallas_call(
        functools.partial(kernel, dp, subs),
        out_shape=shapes,
        in_specs=[hbm] * 3,
        out_specs=(vmem,) * 3,
        scratch_shapes=[
            pltpu.VMEM((2, rows, dim), BF16),
            pltpu.VMEM((width, codes), F32),
            pltpu.VMEM((half, width, dim), BF16),
            pltpu.VMEM((half, width + 16, codes), BF16),
            pltpu.VMEM((2, rows, dim // 2), BF16),
            pltpu.VMEM((2, rows, dim // 2), BF16),
            pltpu.VMEM((half, dp, chunk, LANES), BF16),
            pltpu.VMEM((group, tile, LANES), BF16),
            pltpu.VMEM((group, chunk, LANES), BF16),
            pltpu.VMEM((group, tile, LANES), BF16),
            pltpu.VMEM((dp, chunk, LANES), BF16),
            pltpu.VMEM((4, tile // 2, LANES), F32),
            pltpu.VMEM((dp, chunk, LANES), BF16),
            dma((3,)),
            dma((subs,)),
            dma((half,)),
            dma((subs,)),
            dma((half,)),
            dma((3,)),
            dma((3,)),
            dma((group,)),
            dma((group,)),
            dma((group,)),
            dma((group,)),
            dma((dp,)),
            dma((dp,)),
        ],
        compiler_params=pltpu.CompilerParams(
            collective_id=0, has_side_effects=True, vmem_limit_bytes=40 * 1024 * 1024
        ),
    )(samples, rotation.T, codebook.swapaxes(1, 2))
    recon, new_codes, cross = pl.pallas_call(
        write_kernel,
        out_shape=shapes,
        in_specs=[vmem] * 3,
        out_specs=(hbm,) * 3,
        scratch_shapes=[dma((3,))],
    )(*parts)
    return recon, new_codes.swapaxes(1, 2), cross


def solution(mesh):
    in_specs = (P(("dp", "sub"), None), P(None, "sub"), P("sub", None, None))
    out_specs = (P(("dp", "sub"), None), P("sub", None, None), P(("dp", "sub"), None))
    return jax.shard_map(
        functools.partial(per_device, mesh.shape["dp"], mesh.shape["sub"]),
        mesh=mesh,
        in_specs=in_specs,
        out_specs=out_specs,
        check_vma=False,
    )
```

```python
import functools

import jax
import jax.numpy as jnp
from jax import lax
from jax.experimental import pallas as pl
from jax.experimental.pallas import tpu as pltpu
from jax.sharding import PartitionSpec as P

MESH = pl.DeviceIdType.MESH
F32 = jnp.float32
BF16 = jnp.bfloat16
LANES = 128
NT = (((1,), (1,)), ((), ()))
TN = (((0,), (0,)), ((), ()))


def each(count, body, start=0):
    if count - start <= 32:
        for i in range(start, count):
            body(i)
    else:
        def step(i, carry):
            body(i)
            return carry

        lax.fori_loop(start, count, step, 0)


def kernel(
    dp,
    subs,
    samples_hbm,
    rotation_hbm,
    codebook_hbm,
    recon_ref,
    new_ref,
    cross_ref,
    samples_all,
    code_own,
    rot_all,
    code_all,
    rec_part,
    rec_halves,
    pack_s,
    pack_x,
    two_s,
    two_x,
    spare,
    halves,
    final,
    local_sem,
    rot_send,
    rot_recv,
    code_send,
    code_recv,
    swap_send,
    swap_recv,
    two_s_send,
    two_s_recv,
    two_x_send,
    two_x_recv,
    new_send,
    new_recv,
):
    chips_z = dp // 2
    half = subs // 2
    group = chips_z * subs
    my_dp = lax.axis_index("dp")
    my_sub = lax.axis_index("sub")
    core = lax.rem(my_dp, 2)
    my_z = my_dp // 2
    me = my_z * subs + my_sub
    _, rows, dim = samples_all.shape
    width, codes = code_own.shape
    chunk = codes // dp
    out_rows = cross_ref.shape[0]
    home = my_sub // half == core
    home_index = lax.rem(my_sub, half)

    load_samples = pltpu.make_async_copy(samples_hbm, samples_all.at[core], local_sem.at[0])
    load_codes = pltpu.make_async_copy(codebook_hbm.at[0], code_own, local_sem.at[1])
    load_rotation = pltpu.make_async_copy(rotation_hbm, rot_all.at[home_index], local_sem.at[2])
    load_codes.start()
    load_samples.start()

    @pl.when(home)
    def _():
        load_rotation.start()

    barrier = pltpu.get_barrier_semaphore()
    everyone = dp * subs
    my_id = my_dp * subs + my_sub

    def greet(k):
        n = lax.rem(my_id + k, everyone)
        pl.semaphore_signal(
            barrier, inc=1, device_id=(n // subs, lax.rem(n, subs)), device_id_type=MESH
        )

    each(everyone, greet, 1)

    load_codes.wait()

    @pl.when(home)
    def _():
        code_t = code_own[...]
        square = jnp.sum(code_t * code_t, axis=0, keepdims=True)
        high = square.astype(BF16).astype(F32)
        middle = (square - high).astype(BF16).astype(F32)
        low = square - high - middle
        row = lax.broadcasted_iota(jnp.int32, (16, codes), 0)
        split = jnp.where(
            row == 0, high, jnp.where(row == 1, middle, jnp.where(row == 2, low, 0.0))
        )
        code_all[home_index, 0:width] = code_t.astype(BF16)
        code_all[home_index, width : width + 16] = split.astype(BF16)
        load_rotation.wait()

    load_samples.wait()
    pl.semaphore_wait(barrier, everyone - 1)

    def swap(src, dst, k):
        return pltpu.make_async_remote_copy(
            src_ref=src,
            dst_ref=dst,
            send_sem=swap_send.at[k],
            recv_sem=swap_recv.at[k],
            device_id=(2 * my_z + 1 - core, my_sub),
            device_id_type=MESH,
        )

    def gather_copy(buffer, send, recv, k, index):
        return pltpu.make_async_remote_copy(
            src_ref=buffer.at[index],
            dst_ref=buffer.at[index],
            send_sem=send.at[k],
            recv_sem=recv.at[index],
            device_id=(my_dp, lax.rem(my_sub + k, subs)),
            device_id_type=MESH,
        )

    @pl.when(home)
    def _():
        def send_gather(k):
            gather_copy(rot_all, rot_send, rot_recv, k, home_index).start()
            gather_copy(code_all, code_send, code_recv, k, home_index).start()

        each(subs, send_gather, 1)

    swap_samples = swap(samples_all.at[core], samples_all.at[core], 0)
    swap_samples.start()
    swap_samples.wait_recv()

    samples = samples_all[...].reshape(2 * rows, dim)
    ones = jnp.ones((2 * rows, LANES - width), BF16)

    def spread(src, two, send, recv, n):
        return pltpu.make_async_remote_copy(
            src_ref=src,
            dst_ref=two.at[me],
            send_sem=send.at[n],
            recv_sem=recv.at[me],
            device_id=(2 * (n // subs) + core, lax.rem(n, subs)),
            device_id_type=MESH,
        )

    def arrived(two, send, recv, n):
        return pltpu.make_async_remote_copy(
            src_ref=two.at[n],
            dst_ref=two.at[n],
            send_sem=send.at[n],
            recv_sem=recv.at[n],
            device_id=(2 * (n // subs) + core, lax.rem(n, subs)),
            device_id_type=MESH,
        )

    def chunk_of(n):
        return lax.rem(n, subs) // half * chips_z + n // subs

    def spread_s(n):
        return spread(pack_s.at[lax.rem(n, half), chunk_of(n)], two_s, two_s_send, two_s_recv, n)

    def assign(i):
        @pl.when(jnp.logical_not(jnp.logical_and(home, home_index == i)))
        def _():
            gather_copy(rot_all, rot_send, rot_recv, 1, i).wait_recv()
            gather_copy(code_all, code_send, code_recv, 1, i).wait_recv()

        rotated = lax.dot_general(samples, rot_all[i], NT, preferred_element_type=F32).astype(BF16)
        wide = rotated.astype(F32)
        row_square = jnp.sum(wide * wide, axis=1, keepdims=True)
        code_low = code_all[i, 0:width]
        code_square = jnp.sum(code_all[i, width : width + 16].astype(F32), axis=0, keepdims=True)
        inner = jnp.dot(rotated, code_low, preferred_element_type=F32)
        logits = -0.125 * (row_square - 2.0 * inner + code_square)
        powers = jnp.exp(logits - jnp.max(logits, axis=1, keepdims=True))
        weights = (powers / jnp.sum(powers, axis=1, keepdims=True)).astype(BF16)
        sums = lax.dot_general(
            weights,
            jnp.concatenate([rotated, ones], axis=1),
            TN,
            preferred_element_type=F32,
        ).reshape(dp, chunk, LANES)
        if chunk < 16:
            sums = jnp.concatenate([sums, jnp.zeros((dp, 16 - chunk, LANES), F32)], axis=1)
        pack_s[i] = sums.astype(BF16)

        def send_sums(m):
            n = half * lax.rem(me // half + m, group // half) + i
            if isinstance(m, int) and m > 0:
                spread_s(n).start()
            else:
                pl.when(n != me)(lambda: spread_s(n).start())

        each(group // half, send_sums)
        return lax.dot_general(weights, code_low, NT, preferred_element_type=F32).astype(BF16)

    recon = jnp.concatenate([assign(i) for i in range(half)], axis=1)
    rec_part[...] = recon.reshape(rec_part.shape)
    swap_recon = swap(rec_part.at[1 - core], rec_halves.at[core], 1)
    swap_recon.start()

    cross = lax.dot_general(samples, recon, TN, preferred_element_type=F32)
    cross = cross.reshape(chips_z, 2, subs, out_rows, dim // 2)
    pack_x[...] = (
        jnp.concatenate(
            [cross[:, c, ..., j : j + LANES] for c in range(2) for j in range(0, dim // 2, LANES)],
            axis=2,
        )
        .astype(BF16)
        .reshape(pack_x.shape)
    )

    def spread_x(k):
        n = lax.rem(me + k, group)
        return spread(pack_x.at[n], two_x, two_x_send, two_x_recv, n)

    each(group, lambda k: spread_x(k).start(), 1)
    rec_halves[core] = rec_part[core]
    two_s[me] = pack_s[lax.rem(me, half), chunk_of(me)]
    two_x[me] = pack_x[me]

    def wait_s(k):
        arrived(two_s, two_s_send, two_s_recv, lax.rem(me + k, group)).wait_recv()

    each(group, wait_s, 1)
    mine = chunk_of(me)
    final[mine] = jnp.sum(two_s[...].astype(F32), axis=0).astype(BF16)
    owned = core * half + home_index

    def share(t):
        return pltpu.make_async_remote_copy(
            src_ref=final.at[mine],
            dst_ref=spare.at[mine],
            send_sem=new_send.at[t],
            recv_sem=new_recv.at[mine],
            device_id=(lax.rem(my_dp + t, dp), owned),
            device_id_type=MESH,
        )

    each(dp, lambda t: share(t).start(), 1)

    @pl.when(home)
    def _():
        spare[mine] = final[mine]

    @pl.when(jnp.logical_not(home))
    def _():
        share(0).start()

    def wait_x(k):
        arrived(two_x, two_x_send, two_x_recv, lax.rem(me + k, group)).wait_recv()

    each(group, wait_x, 1)
    total_x = jnp.sum(two_x[...].astype(F32), axis=0)
    tall = total_x.shape[0] // 2
    final_x = total_x.reshape(2, tall, LANES)
    halves[2:4] = final_x
    swap_x = swap(halves.at[3 - core], halves.at[core], 2)
    swap_x.start()
    halves[core] = halves[2 + core]
    swap_recon.wait_recv()
    for c in range(2):
        recon_ref[:, c * (dim // 2) : (c + 1) * (dim // 2)] = rec_halves[c]

    def received(t):
        j = lax.rem(mine + t, dp)
        return pltpu.make_async_remote_copy(
            src_ref=spare.at[j],
            dst_ref=spare.at[j],
            send_sem=new_send.at[0],
            recv_sem=new_recv.at[j],
            device_id=(my_dp, owned),
            device_id_type=MESH,
        )

    swap_x.wait_recv()
    for c in range(2):
        for j in range(dim // 2 // LANES):
            at = c * (dim // 2) + j * LANES
            cross_ref[:, at : at + LANES] = halves[c, j * out_rows : (j + 1) * out_rows]

    each(dp, lambda t: received(t).wait_recv(), 1)

    @pl.when(jnp.logical_not(home))
    def _():
        received(0).wait_recv()

    totals = spare[...].astype(F32)[:, :chunk].reshape(codes, LANES).T
    new_ref[0] = (totals[:width] + code_own[...]) / (totals[width : 2 * width] + 1.0)

    @pl.when(home)
    def _():
        def finish(k):
            gather_copy(rot_all, rot_send, rot_recv, k, home_index).wait_send()
            gather_copy(code_all, code_send, code_recv, k, home_index).wait_send()

        each(subs, finish, 1)

    @pl.when(jnp.logical_not(home))
    def _():
        share(0).wait_send()

    swap_samples.wait_send()
    swap_recon.wait_send()
    swap_x.wait_send()
    each(group, lambda k: spread_s(lax.rem(me + k, group)).wait_send(), 1)
    each(group, lambda k: spread_x(k).wait_send(), 1)
    each(dp, lambda t: share(t).wait_send(), 1)


def write_kernel(recon_ref, new_ref, cross_ref, recon_out, new_out, cross_out, sems):
    pairs = ((recon_ref, recon_out), (new_ref, new_out), (cross_ref, cross_out))
    copies = [pltpu.make_async_copy(s, d, sems.at[i]) for i, (s, d) in enumerate(pairs)]
    for copy in copies:
        copy.start()
    for copy in copies:
        copy.wait()


def per_device(dp, subs, samples, rotation, codebook):
    rows, dim = samples.shape
    codes, width = codebook.shape[1:]
    half = subs // 2
    group = dp // 2 * subs
    chunk = max(16, codes // dp)
    out_rows = dim // (dp * subs)
    tile = out_rows * dim // LANES
    dma = pltpu.SemaphoreType.DMA
    vmem = pl.BlockSpec(memory_space=pltpu.VMEM)
    hbm = pl.BlockSpec(memory_space=pltpu.HBM)
    shapes = (
        jax.ShapeDtypeStruct((rows, dim), BF16),
        jax.ShapeDtypeStruct((1, width, codes), F32),
        jax.ShapeDtypeStruct((out_rows, dim), F32),
    )
    parts = pl.pallas_call(
        functools.partial(kernel, dp, subs),
        out_shape=shapes,
        in_specs=[hbm] * 3,
        out_specs=(vmem,) * 3,
        scratch_shapes=[
            pltpu.VMEM((2, rows, dim), BF16),
            pltpu.VMEM((width, codes), F32),
            pltpu.VMEM((half, width, dim), BF16),
            pltpu.VMEM((half, width + 16, codes), BF16),
            pltpu.VMEM((2, rows, dim // 2), BF16),
            pltpu.VMEM((2, rows, dim // 2), BF16),
            pltpu.VMEM((half, dp, chunk, LANES), BF16),
            pltpu.VMEM((group, tile, LANES), BF16),
            pltpu.VMEM((group, chunk, LANES), BF16),
            pltpu.VMEM((group, tile, LANES), BF16),
            pltpu.VMEM((dp, chunk, LANES), BF16),
            pltpu.VMEM((4, tile // 2, LANES), F32),
            pltpu.VMEM((dp, chunk, LANES), BF16),
            dma((3,)),
            dma((subs,)),
            dma((half,)),
            dma((subs,)),
            dma((half,)),
            dma((3,)),
            dma((3,)),
            dma((group,)),
            dma((group,)),
            dma((group,)),
            dma((group,)),
            dma((dp,)),
            dma((dp,)),
        ],
        compiler_params=pltpu.CompilerParams(
            collective_id=0, has_side_effects=True, vmem_limit_bytes=40 * 1024 * 1024
        ),
    )(*(pltpu.with_memory_space_constraint(x, pltpu.HBM) for x in (samples, rotation.T, codebook.swapaxes(1, 2))))
    recon, new_codes, cross = pl.pallas_call(
        write_kernel,
        out_shape=shapes,
        in_specs=[vmem] * 3,
        out_specs=(hbm,) * 3,
        scratch_shapes=[dma((3,))],
        compiler_params=pltpu.CompilerParams(vmem_limit_bytes=4 * 1024 * 1024),
    )(*parts)
    return recon, new_codes.swapaxes(1, 2), cross


def solution(mesh):
    in_specs = (P(("dp", "sub"), None), P(None, "sub"), P("sub", None, None))
    out_specs = (P(("dp", "sub"), None), P("sub", None, None), P(("dp", "sub"), None))
    return jax.shard_map(
        functools.partial(per_device, mesh.shape["dp"], mesh.shape["sub"]),
        mesh=mesh,
        in_specs=in_specs,
        out_specs=out_specs,
        check_vma=False,
    )
```

```python
import functools

import jax
import jax.numpy as jnp
from jax import lax
from jax.experimental import pallas as pl
from jax.experimental.pallas import tpu as pltpu
from jax.sharding import PartitionSpec as P

MESH = pl.DeviceIdType.MESH
F32 = jnp.float32
BF16 = jnp.bfloat16
LANES = 128
NT = (((1,), (1,)), ((), ()))
TN = (((0,), (0,)), ((), ()))


def each(count, body, start=0):
    if count - start <= 32:
        for i in range(start, count):
            body(i)
    else:
        def step(i, carry):
            body(i)
            return carry

        lax.fori_loop(start, count, step, 0)


def kernel(
    dp,
    subs,
    samples_hbm,
    rotation_hbm,
    codebook_hbm,
    recon_ref,
    new_ref,
    cross_ref,
    samples_all,
    samples_t,
    code_own,
    rot_all,
    code_all,
    rec_part,
    rec_halves,
    pack_s,
    pack_x,
    two_s,
    two_x,
    count_out,
    count_in,
    own_total,
    totals,
    halves,
    local_sem,
    gather_send,
    rot_recv,
    code_recv,
    swap_send,
    swap_recv,
    many_send,
    many_recv,
):
    chips_z = dp // 2
    half = subs // 2
    group = chips_z * subs
    my_dp = lax.axis_index("dp")
    my_sub = lax.axis_index("sub")
    core = lax.rem(my_dp, 2)
    my_z = my_dp // 2
    my_part = my_sub // half
    me = my_z * subs + my_sub
    _, rows, dim = samples_all.shape
    width, codes = code_own.shape
    chunk = width // dp
    out_rows = cross_ref.shape[0]
    home = my_part == core
    home_index = my_sub - my_part * half
    mine = my_part * chips_z + my_z
    owned = core * half + home_index

    def wrap(index, count):
        return jnp.where(index >= count, index - count, index)

    load_samples = pltpu.make_async_copy(samples_hbm, samples_all.at[core], local_sem.at[0])
    load_codes = pltpu.make_async_copy(codebook_hbm.at[0], code_own, local_sem.at[1])
    load_rotation = pltpu.make_async_copy(rotation_hbm, rot_all.at[home_index], local_sem.at[2])

    barrier = pltpu.get_barrier_semaphore()

    def greet(k):
        d = wrap(my_dp + k, dp)
        for j in range(subs):
            if isinstance(k, int) and k == 0 and j == 0:
                continue
            pl.semaphore_signal(
                barrier, inc=1, device_id=(d, wrap(my_sub + j, subs)), device_id_type=MESH
            )

    each(dp, greet)
    load_codes.start()
    load_samples.start()

    @pl.when(home)
    def _():
        load_rotation.start()

    load_codes.wait()

    @pl.when(home)
    def _():
        code_t = code_own[...]
        square = -0.5 * jnp.sum(code_t * code_t, axis=0, keepdims=True)
        high = square.astype(BF16).astype(F32)
        middle = (square - high).astype(BF16).astype(F32)
        low = square - high - middle
        row = lax.broadcasted_iota(jnp.int32, (16, codes), 0)
        split = jnp.where(
            row == 0, high, jnp.where(row == 1, middle, jnp.where(row == 2, low, 0.0))
        )
        code_all[home_index, 0:width] = code_t.astype(BF16)
        code_all[home_index, width : width + 16] = split.astype(BF16)
        load_rotation.wait()

    load_samples.wait()
    pl.semaphore_wait(barrier, dp * subs - 1)

    def remote(src, dst, send, recv, device):
        return pltpu.make_async_remote_copy(
            src_ref=src,
            dst_ref=dst,
            send_sem=send,
            recv_sem=recv,
            device_id=device,
            device_id_type=MESH,
        )

    partner = (my_dp + 1 - 2 * core, my_sub)

    def swap(src, dst, k):
        return remote(src, dst, swap_send.at[k], swap_recv.at[k], partner)

    def rot_copy(index, k, device):
        slot = rot_all.at[index]
        return remote(slot, slot, gather_send.at[k], rot_recv.at[index], device)

    def code_copy(index, k, device):
        slot = code_all.at[index]
        return remote(slot, slot, gather_send.at[subs + k], code_recv.at[index], device)

    def gather_peer(k):
        return (my_dp, wrap(my_sub + k, subs))

    swap_samples = swap(samples_all.at[core], samples_all.at[core], 0)
    swap_samples.start()

    @pl.when(home)
    def _():
        for k in range(1, subs):
            rot_copy(home_index, k, gather_peer(k)).start()
        for k in range(1, subs):
            code_copy(home_index, k, gather_peer(k)).start()

    swap_samples.wait_recv()
    samples_t[...] = samples_all[...].reshape(2 * rows, dim).astype(F32).T.astype(BF16)

    for i in range(half):
        @pl.when(jnp.logical_not(jnp.logical_and(home, home_index == i)))
        def _():
            rot_copy(i, 1, partner).wait_recv()
            code_copy(i, 1, partner).wait_recv()

    rotated_all = jnp.dot(
        rot_all[...].reshape(half * width, dim), samples_t[...], preferred_element_type=F32
    ).astype(BF16)
    ones = jnp.ones((16, 2 * rows), BF16)
    recon = []
    for i in range(half):
        rotated = rotated_all[i * width : (i + 1) * width]
        wide = rotated.astype(F32)
        row_square = jnp.sum(wide * wide, axis=0, keepdims=True)
        tall = jnp.concatenate([rotated, ones], axis=0)
        inner = lax.dot_general(code_all[i], tall, TN, preferred_element_type=F32)
        logits = -0.125 * (row_square - 2.0 * inner)
        powers = jnp.exp(logits - jnp.max(logits, axis=0, keepdims=True))
        weights = (powers * (1.0 / jnp.sum(powers, axis=0, keepdims=True))).astype(BF16)
        sums = lax.dot_general(tall, weights, NT, preferred_element_type=F32)
        count_out[i] = sums[width : width + 1]
        pieces = sums[:width].reshape(dp, chunk, codes)
        pieces = jnp.concatenate(
            [pieces[..., j : j + LANES] for j in range(0, codes, LANES)], axis=1
        )
        fill = pack_s.shape[2] - pieces.shape[1]
        if fill:
            pieces = jnp.concatenate([pieces, jnp.zeros((dp, fill, LANES), F32)], axis=1)
        pack_s[i] = pieces.astype(BF16)
        recon.append(
            jnp.dot(code_all[i, 0:width], weights, preferred_element_type=F32).astype(BF16)
        )

    def each_peer(body):
        def plane(dz):
            z = wrap(my_z + dz, chips_z)
            for p in range(2):
                part = wrap(my_part + p, 2)
                for i in range(half):
                    if isinstance(dz, int) and (dz > 0 or p > 0):
                        body(z, part, i)
                    else:
                        other = jnp.logical_or(i != home_index, jnp.logical_or(dz > 0, p > 0))
                        pl.when(other)(functools.partial(body, z, part, i))

        each(chips_z, plane)

    def send_s(z, part, i):
        remote(
            pack_s.at[i, part * chips_z + z],
            two_s.at[me],
            many_send.at[0],
            many_recv.at[0],
            (2 * z + core, part * half + i),
        ).start()

    def send_x(z, part, i):
        sub = part * half + i
        remote(
            pack_x.at[z * subs + sub],
            two_x.at[me],
            many_send.at[1],
            many_recv.at[1],
            (2 * z + core, sub),
        ).start()

    each_peer(send_s)

    recon = jnp.concatenate(recon, axis=0)
    cross = lax.dot_general(samples_t[...], recon, NT, preferred_element_type=F32)
    cross = cross.reshape(chips_z, 2, subs, out_rows, dim // 2)
    pack_x[...] = (
        jnp.concatenate(
            [cross[:, c, ..., j : j + LANES] for c in range(2) for j in range(0, dim // 2, LANES)],
            axis=2,
        )
        .astype(BF16)
        .reshape(pack_x.shape)
    )
    each_peer(send_x)

    def send_count(t, i):
        return remote(
            count_out.at[i],
            count_in.at[me],
            many_send.at[2],
            many_recv.at[2],
            (wrap(my_dp + t, dp), core * half + i),
        )

    def send_counts(t):
        for i in range(half):
            if isinstance(t, int) and t > 0:
                send_count(t, i).start()
            else:
                self = jnp.logical_and(t == 0, jnp.logical_and(home, home_index == i))
                pl.when(jnp.logical_not(self))(lambda: send_count(t, i).start())

    each(dp, send_counts)

    @pl.when(home)
    def _():
        count_in[me] = count_out[home_index]

    rec_part[...] = recon.astype(F32).T.astype(BF16).reshape(rec_part.shape)
    swap_recon = swap(rec_part.at[1 - core], rec_halves.at[core], 1)
    swap_recon.start()
    rec_halves[core] = rec_part[core]
    two_s[me] = pack_s[home_index, mine]
    two_x[me] = pack_x[me]

    def wait_recv(buffer, count, k):
        part = buffer.at[pl.ds(0, count)]
        remote(part, part, many_send.at[k], many_recv.at[k], partner).wait_recv()

    def wait_send(buffer, count, k):
        part = buffer.at[pl.ds(0, count)]
        remote(part, part, many_send.at[k], many_recv.at[k], partner).wait_send()

    wait_recv(two_s, group - 1, 0)
    own_total[...] = jnp.sum(two_s[...].astype(F32), axis=0).astype(BF16)

    def share(t):
        return remote(
            own_total, totals.at[mine], many_send.at[3], many_recv.at[3], (wrap(my_dp + t, dp), owned)
        )

    each(dp, lambda t: share(t).start(), 1)

    @pl.when(home)
    def _():
        totals[mine] = own_total[...]

    @pl.when(jnp.logical_not(home))
    def _():
        share(0).start()

    wait_recv(two_x, group - 1, 1)
    total_x = jnp.sum(two_x[...].astype(F32), axis=0)
    halves[2:4] = total_x.reshape(2, total_x.shape[0] // 2, LANES)
    swap_x = swap(halves.at[3 - core], halves.at[core], 2)
    swap_x.start()
    halves[core] = halves[2 + core]
    swap_recon.wait_recv()
    for c in range(2):
        recon_ref[:, c * (dim // 2) : (c + 1) * (dim // 2)] = rec_halves[c]
    swap_x.wait_recv()
    for c in range(2):
        for j in range(dim // 2 // LANES):
            at = c * (dim // 2) + j * LANES
            cross_ref[:, at : at + LANES] = halves[c, j * out_rows : (j + 1) * out_rows]

    @pl.when(home)
    def _():
        wait_recv(count_in, group - 1, 2)
        wait_recv(totals, dp - 1, 3)
        wait_send(count_in, group - 1, 2)
        wait_send(totals, dp - 1, 3)
        for k in range(1, subs):
            rot_copy(home_index, k, partner).wait_send()
            code_copy(home_index, k, partner).wait_send()

    @pl.when(jnp.logical_not(home))
    def _():
        wait_recv(count_in, group, 2)
        wait_recv(totals, dp, 3)
        wait_send(count_in, group, 2)
        wait_send(totals, dp, 3)

    counts = jnp.sum(count_in[...], axis=0) + 1.0
    all_totals = totals[...].astype(F32)
    for j in range(codes // LANES):
        lanes = slice(j * LANES, (j + 1) * LANES)
        sums = all_totals[:, j * chunk : (j + 1) * chunk].reshape(width, LANES)
        new_ref[0, :, lanes] = (sums + code_own[:, lanes]) / counts[:, lanes]

    swap_samples.wait_send()
    swap_recon.wait_send()
    swap_x.wait_send()
    wait_send(two_s, group - 1, 0)
    wait_send(two_x, group - 1, 1)


def write_kernel(recon_ref, new_ref, cross_ref, recon_out, new_out, cross_out, sems):
    pairs = ((recon_ref, recon_out), (new_ref, new_out), (cross_ref, cross_out))
    copies = [pltpu.make_async_copy(s, d, sems.at[i]) for i, (s, d) in enumerate(pairs)]
    for copy in copies:
        copy.start()
    for copy in copies:
        copy.wait()


def per_device(dp, subs, samples, rotation, codebook):
    rows, dim = samples.shape
    codes, width = codebook.shape[1:]
    half = subs // 2
    group = dp // 2 * subs
    chunk = max(16, width * codes // (dp * LANES))
    out_rows = dim // (dp * subs)
    tile = out_rows * dim // LANES
    dma = pltpu.SemaphoreType.DMA
    vmem = pl.BlockSpec(memory_space=pltpu.VMEM)
    hbm = pl.BlockSpec(memory_space=pltpu.HBM)
    shapes = (
        jax.ShapeDtypeStruct((rows, dim), BF16),
        jax.ShapeDtypeStruct((1, width, codes), F32),
        jax.ShapeDtypeStruct((out_rows, dim), F32),
    )
    parts = pl.pallas_call(
        functools.partial(kernel, dp, subs),
        out_shape=shapes,
        in_specs=[hbm] * 3,
        out_specs=(vmem,) * 3,
        scratch_shapes=[
            pltpu.VMEM((2, rows, dim), BF16),
            pltpu.VMEM((dim, 2 * rows), BF16),
            pltpu.VMEM((width, codes), F32),
            pltpu.VMEM((half, width, dim), BF16),
            pltpu.VMEM((half, width + 16, codes), BF16),
            pltpu.VMEM((2, rows, dim // 2), BF16),
            pltpu.VMEM((2, rows, dim // 2), BF16),
            pltpu.VMEM((half, dp, chunk, LANES), BF16),
            pltpu.VMEM((group, tile, LANES), BF16),
            pltpu.VMEM((group, chunk, LANES), BF16),
            pltpu.VMEM((group, tile, LANES), BF16),
            pltpu.VMEM((half, 1, codes), F32),
            pltpu.VMEM((group, 1, codes), F32),
            pltpu.VMEM((chunk, LANES), BF16),
            pltpu.VMEM((dp, chunk, LANES), BF16),
            pltpu.VMEM((4, tile // 2, LANES), F32),
            dma((3,)),
            dma((2 * subs,)),
            dma((half,)),
            dma((half,)),
            dma((3,)),
            dma((3,)),
            dma((4,)),
            dma((4,)),
        ],
        compiler_params=pltpu.CompilerParams(
            collective_id=0, has_side_effects=True, vmem_limit_bytes=40 * 1024 * 1024
        ),
    )(
        *(
            pltpu.with_memory_space_constraint(x, pltpu.HBM)
            for x in (samples, rotation.T, codebook.swapaxes(1, 2))
        )
    )
    recon, new_codes, cross = pl.pallas_call(
        write_kernel,
        out_shape=shapes,
        in_specs=[vmem] * 3,
        out_specs=(hbm,) * 3,
        scratch_shapes=[dma((3,))],
        compiler_params=pltpu.CompilerParams(vmem_limit_bytes=4 * 1024 * 1024),
    )(*parts)
    return recon, new_codes.swapaxes(1, 2), cross


def solution(mesh):
    in_specs = (P(("dp", "sub"), None), P(None, "sub"), P("sub", None, None))
    out_specs = (P(("dp", "sub"), None), P("sub", None, None), P(("dp", "sub"), None))
    return jax.shard_map(
        functools.partial(per_device, mesh.shape["dp"], mesh.shape["sub"]),
        mesh=mesh,
        in_specs=in_specs,
        out_specs=out_specs,
        check_vma=False,
    )
```

```python
import functools

import jax
import jax.numpy as jnp
from jax import lax
from jax.experimental import pallas as pl
from jax.experimental.pallas import tpu as pltpu
from jax.sharding import PartitionSpec as P

MESH = pl.DeviceIdType.MESH
F32 = jnp.float32
BF16 = jnp.bfloat16
LANES = 128
NT = (((1,), (1,)), ((), ()))
TN = (((0,), (0,)), ((), ()))


def kernel(
    dp,
    subs,
    samples_hbm,
    rotation_hbm,
    codebook_hbm,
    recon_ref,
    new_ref,
    cross_ref,
    blocks,
    rotation,
    code_own,
    code_tall,
    rec_out,
    rec_in,
    pack_s,
    pack_x,
    two_s,
    two_x,
    count_out,
    count_in,
    own_total,
    totals,
    cross_out,
    cross_in,
    local_sem,
    block_send,
    block_recv,
    many_send,
    many_recv,
):
    half = subs // 2
    my_dp = lax.axis_index("dp")
    my_sub = lax.axis_index("sub")
    my_part = my_sub // half
    my_place = my_sub - my_part * half
    _, rows, dim = blocks.shape
    width, codes = code_own.shape
    chunk = width // dp
    out_rows = cross_ref.shape[0]

    def wrap(index, count):
        return jnp.where(index >= count, index - count, index)

    steps = [(p, q) for p in range(2) for q in range(half)]

    def towards(k):
        p, q = steps[k]
        return wrap(my_part + p, 2) * half + wrap(my_place + q, half)

    def origin(k):
        p, q = steps[k]
        return wrap(my_part + 2 - p, 2) * half + wrap(my_place + half - q, half)

    def along(t):
        return wrap(my_dp + t, dp)

    barrier = pltpu.get_barrier_semaphore()
    for k in range(1, subs):
        pl.semaphore_signal(barrier, inc=1, device_id=(my_dp, towards(k)), device_id_type=MESH)
    for t in range(1, dp):
        pl.semaphore_signal(barrier, inc=1, device_id=(along(t), my_sub), device_id_type=MESH)

    load_samples = pltpu.make_async_copy(samples_hbm, blocks.at[0], local_sem.at[0])
    load_codes = pltpu.make_async_copy(codebook_hbm.at[0], code_own, local_sem.at[1])
    load_rotation = pltpu.make_async_copy(rotation_hbm, rotation, local_sem.at[2])
    load_codes.start()
    load_samples.start()
    load_rotation.start()

    def remote(src, dst, send, recv, device):
        return pltpu.make_async_remote_copy(
            src_ref=src,
            dst_ref=dst,
            send_sem=send,
            recv_sem=recv,
            device_id=device,
            device_id_type=MESH,
        )

    def block_copy(k):
        return remote(
            samples_hbm, blocks.at[k], block_send.at[k], block_recv.at[k], (my_dp, towards(k))
        )

    pl.semaphore_wait(barrier, subs + dp - 2)
    for k in range(1, subs):
        block_copy(k).start()

    load_codes.wait()
    code_t = code_own[...]
    square = -0.5 * jnp.sum(code_t * code_t, axis=0, keepdims=True)
    high = square.astype(BF16).astype(F32)
    middle = (square - high).astype(BF16).astype(F32)
    low = square - high - middle
    row = lax.broadcasted_iota(jnp.int32, (16, codes), 0)
    split = jnp.where(row == 0, high, jnp.where(row == 1, middle, jnp.where(row == 2, low, 0.0)))
    code_tall[...] = jnp.concatenate([code_t, split], axis=0).T.astype(BF16)
    code_low = code_t.astype(BF16)
    load_rotation.wait()
    load_samples.wait()
    ones = jnp.ones((16, rows), BF16)

    sums = None
    cross = None
    for k in range(subs):
        if k > 0:
            block_copy(k).wait_recv()
        block = blocks[k]
        rotated = lax.dot_general(rotation[...], block, NT, preferred_element_type=F32).astype(BF16)
        wide = rotated.astype(F32)
        row_square = jnp.sum(wide * wide, axis=0, keepdims=True)
        tall = jnp.concatenate([rotated, ones], axis=0)
        inner = jnp.dot(code_tall[...], tall, preferred_element_type=F32)
        logits = -0.125 * (row_square - 2.0 * inner)
        powers = jnp.exp(logits - jnp.max(logits, axis=0, keepdims=True))
        weights = (powers * (1.0 / jnp.sum(powers, axis=0, keepdims=True))).astype(BF16)
        part = lax.dot_general(tall, weights, NT, preferred_element_type=F32)
        sums = part if sums is None else sums + part
        recon = jnp.dot(code_low, weights, preferred_element_type=F32).astype(BF16)
        part = jnp.dot(recon, block, preferred_element_type=F32)
        cross = part if cross is None else cross + part
        if k == 0:
            rec_in[my_sub] = recon
        else:
            rec_out[k] = recon

    pieces = sums[:width].reshape(dp, chunk, codes)
    pieces = jnp.concatenate([pieces[..., j : j + LANES] for j in range(0, codes, LANES)], axis=1)
    fill = pack_s.shape[1] - pieces.shape[1]
    if fill:
        pieces = jnp.concatenate([pieces, jnp.zeros((dp, fill, LANES), F32)], axis=1)
    pack_s[...] = pieces.astype(BF16)

    def spread(pack, two, t, s):
        return remote(
            pack.at[along(t)], two.at[t - 1], many_send.at[s], many_recv.at[s], (along(t), my_sub)
        )

    for t in range(1, dp):
        spread(pack_s, two_s, t, 0).start()

    tile = pack_x.shape[1]
    pieces = cross.T.reshape(dp, 2, tile, width)
    pack_x[...] = jnp.concatenate([pieces[:, 0], pieces[:, 1]], axis=2).astype(BF16)
    for t in range(1, dp):
        spread(pack_x, two_x, t, 1).start()

    count_out[...] = sums[width : width + 1]

    def send_count(t):
        return remote(
            count_out, count_in.at[my_dp], many_send.at[2], many_recv.at[2], (along(t), my_sub)
        )

    for t in range(1, dp):
        send_count(t).start()
    count_in[my_dp] = count_out[...]

    def send_recon(k):
        device = (my_dp, origin(k))
        return remote(rec_out.at[k], rec_in.at[my_sub], many_send.at[3], many_recv.at[3], device)

    for k in range(1, subs):
        send_recon(k).start()

    def bulk(buffer, count, s):
        part = buffer.at[pl.ds(0, count)]
        return remote(part, part, many_send.at[s], many_recv.at[s], (along(1), my_sub))

    bulk(two_s, dp - 1, 0).wait_recv()
    total = pack_s[my_dp].astype(F32) + jnp.sum(two_s[...].astype(F32), axis=0)
    own_total[...] = total.astype(BF16)

    def share(t):
        return remote(
            own_total, totals.at[my_dp], many_send.at[4], many_recv.at[4], (along(t), my_sub)
        )

    for t in range(1, dp):
        share(t).start()
    totals[my_dp] = own_total[...]

    bulk(two_x, dp - 1, 1).wait_recv()
    total_x = pack_x[my_dp].astype(F32) + jnp.sum(two_x[...].astype(F32), axis=0)
    total_x = jnp.concatenate([total_x[:, :width], total_x[:, width : 2 * width]], axis=0)
    cross_out[...] = jnp.concatenate([total_x, total_x], axis=1).reshape(cross_out.shape)

    def send_cross(k):
        peer = towards(k)
        return remote(
            cross_out.at[peer], cross_in.at[my_sub], many_send.at[5], many_recv.at[5], (my_dp, peer)
        )

    for k in range(1, subs):
        send_cross(k).start()
    cross_in[my_sub] = cross_out[my_sub]

    bulk(rec_in, subs - 1, 3).wait_recv()
    recon_ref[...] = rec_in[...].reshape(dim, rows).astype(F32).T.astype(BF16)

    bulk(count_in, dp - 1, 2).wait_recv()
    counts = 1.0 + jnp.sum(count_in[...], axis=0)
    bulk(totals, dp - 1, 4).wait_recv()
    all_totals = totals[...].astype(F32)
    for j in range(codes // LANES):
        lanes = slice(j * LANES, (j + 1) * LANES)
        part = all_totals[:, j * chunk : (j + 1) * chunk].reshape(width, LANES)
        new_ref[0, :, lanes] = (part + code_own[:, lanes]) / counts[:, lanes]

    bulk(cross_in, subs - 1, 5).wait_recv()
    cross_ref[...] = jnp.concatenate([cross_in[s][:, :width] for s in range(subs)], axis=1)

    for k in range(1, subs):
        block_copy(k).wait_send()
    bulk(two_s, dp - 1, 0).wait_send()
    bulk(two_x, dp - 1, 1).wait_send()
    bulk(count_in, dp - 1, 2).wait_send()
    bulk(rec_in, subs - 1, 3).wait_send()
    bulk(totals, dp - 1, 4).wait_send()
    bulk(cross_in, subs - 1, 5).wait_send()


def write_kernel(recon_ref, new_ref, cross_ref, recon_out, new_out, cross_out, sems):
    pairs = ((recon_ref, recon_out), (new_ref, new_out), (cross_ref, cross_out))
    copies = [pltpu.make_async_copy(s, d, sems.at[i]) for i, (s, d) in enumerate(pairs)]
    for copy in copies:
        copy.start()
    for copy in copies:
        copy.wait()


def per_device(dp, subs, samples, rotation, codebook):
    rows, dim = samples.shape
    codes, width = codebook.shape[1:]
    chunk = max(16, width * codes // (dp * LANES))
    out_rows = dim // (dp * subs)
    tile = dim // dp // 2
    dma = pltpu.SemaphoreType.DMA
    vmem = pl.BlockSpec(memory_space=pltpu.VMEM)
    hbm = pl.BlockSpec(memory_space=pltpu.HBM)
    shapes = (
        jax.ShapeDtypeStruct((rows, dim), BF16),
        jax.ShapeDtypeStruct((1, width, codes), F32),
        jax.ShapeDtypeStruct((out_rows, dim), F32),
    )
    parts = pl.pallas_call(
        functools.partial(kernel, dp, subs),
        out_shape=shapes,
        in_specs=[hbm] * 3,
        out_specs=(vmem,) * 3,
        scratch_shapes=[
            pltpu.VMEM((subs, rows, dim), BF16),
            pltpu.VMEM((width, dim), BF16),
            pltpu.VMEM((width, codes), F32),
            pltpu.VMEM((codes, width + 16), BF16),
            pltpu.VMEM((subs, width, rows), BF16),
            pltpu.VMEM((subs, width, rows), BF16),
            pltpu.VMEM((dp, chunk, LANES), BF16),
            pltpu.VMEM((dp, tile, LANES), BF16),
            pltpu.VMEM((dp - 1, chunk, LANES), BF16),
            pltpu.VMEM((dp - 1, tile, LANES), BF16),
            pltpu.VMEM((1, codes), F32),
            pltpu.VMEM((dp, 1, codes), F32),
            pltpu.VMEM((chunk, LANES), BF16),
            pltpu.VMEM((dp, chunk, LANES), BF16),
            pltpu.VMEM((subs, out_rows, LANES), F32),
            pltpu.VMEM((subs, out_rows, LANES), F32),
            dma((3,)),
            dma((subs,)),
            dma((subs,)),
            dma((6,)),
            dma((6,)),
        ],
        compiler_params=pltpu.CompilerParams(
            collective_id=0, has_side_effects=True, vmem_limit_bytes=40 * 1024 * 1024
        ),
    )(
        *(
            pltpu.with_memory_space_constraint(x, pltpu.HBM)
            for x in (samples, rotation.T, codebook.swapaxes(1, 2))
        )
    )
    recon, new_codes, cross = pl.pallas_call(
        write_kernel,
        out_shape=shapes,
        in_specs=[vmem] * 3,
        out_specs=(hbm,) * 3,
        scratch_shapes=[dma((3,))],
        compiler_params=pltpu.CompilerParams(vmem_limit_bytes=4 * 1024 * 1024),
    )(*parts)
    return recon, new_codes.swapaxes(1, 2), cross


def solution(mesh):
    in_specs = (P(("dp", "sub"), None), P(None, "sub"), P("sub", None, None))
    out_specs = (P(("dp", "sub"), None), P("sub", None, None), P(("dp", "sub"), None))
    return jax.shard_map(
        functools.partial(per_device, mesh.shape["dp"], mesh.shape["sub"]),
        mesh=mesh,
        in_specs=in_specs,
        out_specs=out_specs,
        check_vma=False,
    )
```

```python
import functools

import jax
import jax.numpy as jnp
from jax import lax
from jax.experimental import pallas as pl
from jax.experimental.pallas import tpu as pltpu
from jax.sharding import PartitionSpec as P

MESH = pl.DeviceIdType.MESH
F32 = jnp.float32
BF16 = jnp.bfloat16
LANES = 128
NT = (((1,), (1,)), ((), ()))
TN = (((0,), (0,)), ((), ()))


def kernel(
    dp,
    subs,
    samples_hbm,
    rotation_hbm,
    codebook_hbm,
    recon_ref,
    new_ref,
    cross_ref,
    blocks,
    rotation,
    code_own,
    code_tall,
    rec_out,
    rec_in,
    pack_s,
    pack_x,
    two_s,
    two_x,
    count_out,
    count_in,
    own_total,
    totals,
    cross_out,
    cross_in,
    local_sem,
    block_send,
    block_recv,
    many_send,
    many_recv,
):
    half = subs // 2
    my_dp = lax.axis_index("dp")
    my_sub = lax.axis_index("sub")
    my_part = my_sub // half
    my_place = my_sub - my_part * half
    _, rows, dim = blocks.shape
    width, codes = code_own.shape
    chunk = width // dp
    out_rows = cross_ref.shape[0]

    def wrap(index, count):
        return jnp.where(index >= count, index - count, index)

    steps = [(p, q) for p in range(2) for q in range(half)]

    def towards(k):
        p, q = steps[k]
        return wrap(my_part + p, 2) * half + wrap(my_place + q, half)

    def origin(k):
        p, q = steps[k]
        return wrap(my_part + 2 - p, 2) * half + wrap(my_place + half - q, half)

    def along(t):
        return wrap(my_dp + t, dp)

    barrier = pltpu.get_barrier_semaphore()
    for k in range(1, subs):
        pl.semaphore_signal(barrier, inc=1, device_id=(my_dp, towards(k)), device_id_type=MESH)
    for t in range(1, dp):
        pl.semaphore_signal(barrier, inc=1, device_id=(along(t), my_sub), device_id_type=MESH)

    load_samples = pltpu.make_async_copy(samples_hbm, blocks.at[0], local_sem.at[0])
    load_codes = pltpu.make_async_copy(codebook_hbm.at[0], code_own, local_sem.at[1])
    load_rotation = pltpu.make_async_copy(rotation_hbm, rotation, local_sem.at[2])
    load_codes.start()
    load_samples.start()
    load_rotation.start()

    def remote(src, dst, send, recv, device):
        return pltpu.make_async_remote_copy(
            src_ref=src,
            dst_ref=dst,
            send_sem=send,
            recv_sem=recv,
            device_id=device,
            device_id_type=MESH,
        )

    def block_copy(k):
        return remote(
            blocks.at[0], blocks.at[k], block_send.at[k], block_recv.at[k], (my_dp, towards(k))
        )

    load_samples.wait()
    pl.semaphore_wait(barrier, subs + dp - 2)
    for k in range(1, subs):
        block_copy(k).start()

    load_codes.wait()
    code_t = code_own[...]
    square = -0.5 * jnp.sum(code_t * code_t, axis=0, keepdims=True)
    high = square.astype(BF16).astype(F32)
    middle = (square - high).astype(BF16).astype(F32)
    low = square - high - middle
    row = lax.broadcasted_iota(jnp.int32, (16, codes), 0)
    split = jnp.where(row == 0, high, jnp.where(row == 1, middle, jnp.where(row == 2, low, 0.0)))
    code_tall[...] = jnp.concatenate([code_t, split], axis=0).T.astype(BF16)
    code_low = code_t.astype(BF16)
    load_rotation.wait()

    def assign(first, count):
        for k in range(max(first, 1), first + count):
            block_copy(k).wait_recv()
        block = blocks[first : first + count].reshape(count * rows, dim)
        rotated = lax.dot_general(rotation[...], block, NT, preferred_element_type=F32).astype(BF16)
        wide = rotated.astype(F32)
        row_square = jnp.sum(wide * wide, axis=0, keepdims=True)
        tall = jnp.concatenate([rotated, jnp.ones((16, count * rows), BF16)], axis=0)
        inner = jnp.dot(code_tall[...], tall, preferred_element_type=F32)
        logits = -0.125 * (row_square - 2.0 * inner)
        powers = jnp.exp(logits - jnp.max(logits, axis=0, keepdims=True))
        weights = (powers * (1.0 / jnp.sum(powers, axis=0, keepdims=True))).astype(BF16)
        return weights, lax.dot_general(tall, weights, NT, preferred_element_type=F32), block

    def rebuild(first, count, weights, block):
        recon = jnp.dot(code_low, weights, preferred_element_type=F32).astype(BF16)
        for k in range(first, first + count):
            piece = recon[:, (k - first) * rows : (k - first + 1) * rows]
            if k == 0:
                rec_in[my_sub] = piece
            else:
                rec_out[k] = piece
        return jnp.dot(recon, block, preferred_element_type=F32)

    groups = [(0, 1), (1, 1)] + [(k, 2) for k in range(2, subs, 2)]
    sums = jnp.zeros((width + 16, codes), F32)
    cross = jnp.zeros((width, dim), F32)
    for first, count in groups[:-1]:
        weights, part, block = assign(first, count)
        sums += part
        cross += rebuild(first, count, weights, block)
    weights, part, block = assign(*groups[-1])
    sums += part

    pieces = sums[:width].reshape(dp, chunk, codes)
    pieces = jnp.concatenate([pieces[..., j : j + LANES] for j in range(0, codes, LANES)], axis=1)
    fill = pack_s.shape[1] - pieces.shape[1]
    if fill:
        pieces = jnp.concatenate([pieces, jnp.zeros((dp, fill, LANES), F32)], axis=1)
    pack_s[...] = pieces.astype(BF16)

    def spread(pack, two, t, s):
        return remote(
            pack.at[along(t)], two.at[t - 1], many_send.at[s], many_recv.at[s], (along(t), my_sub)
        )

    for t in range(1, dp):
        spread(pack_s, two_s, t, 0).start()

    cross += rebuild(*groups[-1], weights, block)
    tile = pack_x.shape[1]
    pieces = cross.T.reshape(dp, 2, tile, width)
    pack_x[...] = jnp.concatenate([pieces[:, 0], pieces[:, 1]], axis=2).astype(BF16)
    for t in range(1, dp):
        spread(pack_x, two_x, t, 1).start()

    count_out[...] = sums[width : width + 1]

    def send_count(t):
        return remote(
            count_out, count_in.at[my_dp], many_send.at[2], many_recv.at[2], (along(t), my_sub)
        )

    for t in range(1, dp):
        send_count(t).start()
    count_in[my_dp] = count_out[...]

    def send_recon(k):
        device = (my_dp, origin(k))
        return remote(rec_out.at[k], rec_in.at[my_sub], many_send.at[3], many_recv.at[3], device)

    for k in range(1, subs):
        send_recon(k).start()

    def bulk(buffer, count, s):
        part = buffer.at[pl.ds(0, count)]
        return remote(part, part, many_send.at[s], many_recv.at[s], (along(1), my_sub))

    bulk(two_s, dp - 1, 0).wait_recv()
    total = pack_s[my_dp].astype(F32) + jnp.sum(two_s[...].astype(F32), axis=0)
    own_total[...] = total.astype(BF16)

    def share(t):
        return remote(
            own_total, totals.at[my_dp], many_send.at[4], many_recv.at[4], (along(t), my_sub)
        )

    for t in range(1, dp):
        share(t).start()
    totals[my_dp] = own_total[...]

    bulk(two_x, dp - 1, 1).wait_recv()
    total_x = pack_x[my_dp].astype(F32) + jnp.sum(two_x[...].astype(F32), axis=0)
    total_x = jnp.concatenate([total_x[:, :width], total_x[:, width : 2 * width]], axis=0)
    cross_out[...] = jnp.concatenate([total_x, total_x], axis=1).reshape(cross_out.shape)

    def send_cross(k):
        peer = towards(k)
        return remote(
            cross_out.at[peer], cross_in.at[my_sub], many_send.at[5], many_recv.at[5], (my_dp, peer)
        )

    for k in range(1, subs):
        send_cross(k).start()
    cross_in[my_sub] = cross_out[my_sub]

    bulk(rec_in, subs - 1, 3).wait_recv()
    recon_ref[...] = rec_in[...].reshape(dim, rows).astype(F32).T.astype(BF16)

    bulk(count_in, dp - 1, 2).wait_recv()
    counts = 1.0 + jnp.sum(count_in[...], axis=0)
    bulk(totals, dp - 1, 4).wait_recv()
    all_totals = totals[...].astype(F32)
    for j in range(codes // LANES):
        lanes = slice(j * LANES, (j + 1) * LANES)
        part = all_totals[:, j * chunk : (j + 1) * chunk].reshape(width, LANES)
        new_ref[0, :, lanes] = (part + code_own[:, lanes]) / counts[:, lanes]

    bulk(cross_in, subs - 1, 5).wait_recv()
    cross_ref[...] = jnp.concatenate([cross_in[s][:, :width] for s in range(subs)], axis=1)

    for k in range(1, subs):
        block_copy(k).wait_send()
    bulk(two_s, dp - 1, 0).wait_send()
    bulk(two_x, dp - 1, 1).wait_send()
    bulk(count_in, dp - 1, 2).wait_send()
    bulk(rec_in, subs - 1, 3).wait_send()
    bulk(totals, dp - 1, 4).wait_send()
    bulk(cross_in, subs - 1, 5).wait_send()


def write_kernel(recon_ref, new_ref, cross_ref, recon_out, new_out, cross_out, sems):
    pairs = ((recon_ref, recon_out), (new_ref, new_out), (cross_ref, cross_out))
    copies = [pltpu.make_async_copy(s, d, sems.at[i]) for i, (s, d) in enumerate(pairs)]
    for copy in copies:
        copy.start()
    for copy in copies:
        copy.wait()


def per_device(dp, subs, samples, rotation, codebook):
    rows, dim = samples.shape
    codes, width = codebook.shape[1:]
    chunk = max(16, width * codes // (dp * LANES))
    out_rows = dim // (dp * subs)
    tile = dim // dp // 2
    dma = pltpu.SemaphoreType.DMA
    vmem = pl.BlockSpec(memory_space=pltpu.VMEM)
    hbm = pl.BlockSpec(memory_space=pltpu.HBM)
    shapes = (
        jax.ShapeDtypeStruct((rows, dim), BF16),
        jax.ShapeDtypeStruct((1, width, codes), F32),
        jax.ShapeDtypeStruct((out_rows, dim), F32),
    )
    parts = pl.pallas_call(
        functools.partial(kernel, dp, subs),
        out_shape=shapes,
        in_specs=[hbm] * 3,
        out_specs=(vmem,) * 3,
        scratch_shapes=[
            pltpu.VMEM((subs, rows, dim), BF16),
            pltpu.VMEM((width, dim), BF16),
            pltpu.VMEM((width, codes), F32),
            pltpu.VMEM((codes, width + 16), BF16),
            pltpu.VMEM((subs, width, rows), BF16),
            pltpu.VMEM((subs, width, rows), BF16),
            pltpu.VMEM((dp, chunk, LANES), BF16),
            pltpu.VMEM((dp, tile, LANES), BF16),
            pltpu.VMEM((dp - 1, chunk, LANES), BF16),
            pltpu.VMEM((dp - 1, tile, LANES), BF16),
            pltpu.VMEM((1, codes), F32),
            pltpu.VMEM((dp, 1, codes), F32),
            pltpu.VMEM((chunk, LANES), BF16),
            pltpu.VMEM((dp, chunk, LANES), BF16),
            pltpu.VMEM((subs, out_rows, LANES), F32),
            pltpu.VMEM((subs, out_rows, LANES), F32),
            dma((3,)),
            dma((subs,)),
            dma((subs,)),
            dma((6,)),
            dma((6,)),
        ],
        compiler_params=pltpu.CompilerParams(
            collective_id=0, has_side_effects=True, vmem_limit_bytes=40 * 1024 * 1024
        ),
    )(
        *(
            pltpu.with_memory_space_constraint(x, pltpu.HBM)
            for x in (samples, rotation.T, codebook.swapaxes(1, 2))
        )
    )
    recon, new_codes, cross = pl.pallas_call(
        write_kernel,
        out_shape=shapes,
        in_specs=[vmem] * 3,
        out_specs=(hbm,) * 3,
        scratch_shapes=[dma((3,))],
        compiler_params=pltpu.CompilerParams(vmem_limit_bytes=4 * 1024 * 1024),
    )(*parts)
    return recon, new_codes.swapaxes(1, 2), cross


def solution(mesh):
    in_specs = (P(("dp", "sub"), None), P(None, "sub"), P("sub", None, None))
    out_specs = (P(("dp", "sub"), None), P("sub", None, None), P(("dp", "sub"), None))
    return jax.shard_map(
        functools.partial(per_device, mesh.shape["dp"], mesh.shape["sub"]),
        mesh=mesh,
        in_specs=in_specs,
        out_specs=out_specs,
        check_vma=False,
    )
```

```python
import functools

import jax
import jax.numpy as jnp
from jax import lax
from jax.experimental import pallas as pl
from jax.experimental.pallas import tpu as pltpu
from jax.sharding import PartitionSpec as P

MESH = pl.DeviceIdType.MESH
F32 = jnp.float32
BF16 = jnp.bfloat16
LANES = 128
NT = (((1,), (1,)), ((), ()))
TN = (((0,), (0,)), ((), ()))


def kernel(
    dp,
    subs,
    samples_hbm,
    rotation_hbm,
    codebook_hbm,
    recon_ref,
    new_ref,
    cross_ref,
    blocks,
    rotation,
    code_own,
    code_tall,
    rec_out,
    rec_in,
    pack_s,
    pack_x,
    one_s,
    comb_s,
    two_s,
    two_x,
    count_out,
    count_in,
    new_all,
    cross_out,
    cross_in,
    local_sem,
    block_send,
    block_recv,
    many_send,
    many_recv,
):
    half = subs // 2
    my_dp = lax.axis_index("dp")
    my_sub = lax.axis_index("sub")
    my_part = my_sub // half
    my_place = my_sub - my_part * half
    _, rows, dim = blocks.shape
    width, codes = code_own.shape
    out_rows = cross_ref.shape[0]

    def wrap(index, count):
        return jnp.where(index >= count, index - count, index)

    steps = [(p, q) for p in range(2) for q in range(half)]

    def towards(k):
        p, q = steps[k]
        return wrap(my_part + p, 2) * half + wrap(my_place + q, half)

    def origin(k):
        p, q = steps[k]
        return wrap(my_part + 2 - p, 2) * half + wrap(my_place + half - q, half)

    def along(t):
        return wrap(my_dp + t, dp)

    barrier = pltpu.get_barrier_semaphore()
    for k in range(1, subs):
        pl.semaphore_signal(barrier, inc=1, device_id=(my_dp, towards(k)), device_id_type=MESH)
    for t in range(1, dp):
        pl.semaphore_signal(barrier, inc=1, device_id=(along(t), my_sub), device_id_type=MESH)

    load_samples = pltpu.make_async_copy(samples_hbm, blocks.at[0], local_sem.at[0])
    load_codes = pltpu.make_async_copy(codebook_hbm.at[0], code_own, local_sem.at[1])
    load_rotation = pltpu.make_async_copy(rotation_hbm, rotation, local_sem.at[2])
    load_codes.start()
    load_samples.start()
    load_rotation.start()

    def remote(src, dst, send, recv, device):
        return pltpu.make_async_remote_copy(
            src_ref=src,
            dst_ref=dst,
            send_sem=send,
            recv_sem=recv,
            device_id=device,
            device_id_type=MESH,
        )

    def block_copy(k):
        return remote(
            blocks.at[0], blocks.at[k], block_send.at[k], block_recv.at[k], (my_dp, towards(k))
        )

    load_samples.wait()
    pl.semaphore_wait(barrier, subs + dp - 2)
    for k in range(subs - 1, 0, -1):
        block_copy(k).start()

    load_codes.wait()
    code_t = code_own[...]
    square = -0.5 * jnp.sum(code_t * code_t, axis=0, keepdims=True)
    high = square.astype(BF16).astype(F32)
    middle = (square - high).astype(BF16).astype(F32)
    low = square - high - middle
    row = lax.broadcasted_iota(jnp.int32, (16, codes), 0)
    split = jnp.where(row == 0, high, jnp.where(row == 1, middle, jnp.where(row == 2, low, 0.0)))
    code_tall[...] = jnp.concatenate([code_t, split], axis=0).T.astype(BF16)
    code_low = code_t.astype(BF16)
    load_rotation.wait()

    def assign(first, count):
        for k in range(max(first, 1), first + count):
            block_copy(k).wait_recv()
        block = blocks[first : first + count].reshape(count * rows, dim)
        rotated = lax.dot_general(rotation[...], block, NT, preferred_element_type=F32).astype(BF16)
        wide = rotated.astype(F32)
        row_square = jnp.sum(wide * wide, axis=0, keepdims=True)
        tall = jnp.concatenate([rotated, jnp.ones((16, count * rows), BF16)], axis=0)
        inner = jnp.dot(code_tall[...], tall, preferred_element_type=F32)
        logits = -0.125 * (row_square - 2.0 * inner)
        powers = jnp.exp(logits - jnp.max(logits, axis=0, keepdims=True))
        weights = (powers * (1.0 / jnp.sum(powers, axis=0, keepdims=True))).astype(BF16)
        return weights, lax.dot_general(tall, weights, NT, preferred_element_type=F32), block

    def rebuild(first, count, weights, block):
        recon = jnp.dot(code_low, weights, preferred_element_type=F32).astype(BF16)
        for k in range(first, first + count):
            piece = recon[:, (k - first) * rows : (k - first + 1) * rows]
            if k == 0:
                rec_in[my_sub] = piece
            else:
                rec_out[k] = piece
        return jnp.dot(recon, block, preferred_element_type=F32)

    groups = [(0, 1), (1, 1)] + [(k, 2) for k in range(2, subs, 2)]
    sums = jnp.zeros((width + 16, codes), F32)
    cross = jnp.zeros((width, dim), F32)
    for first, count in groups[:-1]:
        weights, part, block = assign(first, count)
        sums += part
        cross += rebuild(first, count, weights, block)
    weights, part, block = assign(*groups[-1])
    sums += part

    core = lax.rem(my_dp, 2)
    my_z = my_dp // 2
    partner = (my_dp + 1 - 2 * core, my_sub)
    pack_s[...] = sums[:width].astype(BF16).reshape(pack_s.shape)
    swap_s = remote(pack_s.at[1 - core], one_s, many_send.at[4], many_recv.at[4], partner)
    swap_s.start()

    count_out[...] = sums[width : width + 1]

    def send_count(t):
        return remote(
            count_out, count_in.at[my_dp], many_send.at[2], many_recv.at[2], (along(t), my_sub)
        )

    for t in range(1, dp):
        send_count(t).start()
    count_in[my_dp] = count_out[...]

    cross += rebuild(*groups[-1], weights, block)

    swap_s.wait_recv()
    comb_s[...] = (pack_s[core].astype(F32) + one_s[...].astype(F32)).astype(BF16)

    def spread_s(t):
        device = (2 * wrap(my_z + t, dp // 2) + core, my_sub)
        return remote(comb_s, two_s.at[my_z], many_send.at[0], many_recv.at[0], device)

    for t in range(1, dp // 2):
        spread_s(t).start()
    two_s[my_z] = comb_s[...]

    def spread(pack, two, t, s):
        return remote(
            pack.at[along(t)], two.at[t - 1], many_send.at[s], many_recv.at[s], (along(t), my_sub)
        )

    tile = pack_x.shape[1]
    pieces = cross.T.reshape(dp, 2, tile, width)
    pack_x[...] = jnp.concatenate([pieces[:, 0], pieces[:, 1]], axis=2).astype(BF16)
    for t in range(1, dp):
        spread(pack_x, two_x, t, 1).start()

    def send_recon(k):
        device = (my_dp, origin(k))
        return remote(rec_out.at[k], rec_in.at[my_sub], many_send.at[3], many_recv.at[3], device)

    for k in range(1, subs):
        send_recon(k).start()

    def bulk(buffer, count, s):
        part = buffer.at[pl.ds(0, count)]
        return remote(part, part, many_send.at[s], many_recv.at[s], (along(1), my_sub))

    bulk(count_in, dp - 1, 2).wait_recv()
    counts = 1.0 + jnp.sum(count_in[...], axis=0)
    bulk(two_s, dp // 2 - 1, 0).wait_recv()
    mine = pl.ds(pl.multiple_of(core * (width // 2), width // 2), width // 2)
    new_all[core] = (jnp.sum(two_s[...].astype(F32), axis=0) + code_own[mine]) / counts
    swap_new = remote(
        new_all.at[core], new_all.at[core], many_send.at[6], many_recv.at[6], partner
    )
    swap_new.start()

    bulk(two_x, dp - 1, 1).wait_recv()
    total_x = pack_x[my_dp].astype(F32) + jnp.sum(two_x[...].astype(F32), axis=0)
    total_x = jnp.concatenate([total_x[:, :width], total_x[:, width : 2 * width]], axis=0)
    cross_out[...] = jnp.concatenate([total_x, total_x], axis=1).reshape(cross_out.shape)

    def send_cross(k):
        peer = towards(k)
        return remote(
            cross_out.at[peer], cross_in.at[my_sub], many_send.at[5], many_recv.at[5], (my_dp, peer)
        )

    for k in range(1, subs):
        send_cross(k).start()
    cross_in[my_sub] = cross_out[my_sub]

    bulk(rec_in, subs - 1, 3).wait_recv()
    recon_ref[...] = rec_in[...].reshape(dim, rows).astype(F32).T.astype(BF16)

    swap_new.wait_recv()
    new_ref[0] = new_all[...].reshape(width, codes)

    bulk(cross_in, subs - 1, 5).wait_recv()
    cross_ref[...] = jnp.concatenate([cross_in[s][:, :width] for s in range(subs)], axis=1)

    for k in range(1, subs):
        block_copy(k).wait_send()
    swap_s.wait_send()
    swap_new.wait_send()
    bulk(two_s, dp // 2 - 1, 0).wait_send()
    bulk(two_x, dp - 1, 1).wait_send()
    bulk(count_in, dp - 1, 2).wait_send()
    bulk(rec_in, subs - 1, 3).wait_send()
    bulk(cross_in, subs - 1, 5).wait_send()


def write_kernel(recon_ref, new_ref, cross_ref, recon_out, new_out, cross_out, sems):
    pairs = ((recon_ref, recon_out), (new_ref, new_out), (cross_ref, cross_out))
    copies = [pltpu.make_async_copy(s, d, sems.at[i]) for i, (s, d) in enumerate(pairs)]
    for copy in copies:
        copy.start()
    for copy in copies:
        copy.wait()


def per_device(dp, subs, samples, rotation, codebook):
    rows, dim = samples.shape
    codes, width = codebook.shape[1:]
    out_rows = dim // (dp * subs)
    tile = dim // dp // 2
    dma = pltpu.SemaphoreType.DMA
    vmem = pl.BlockSpec(memory_space=pltpu.VMEM)
    hbm = pl.BlockSpec(memory_space=pltpu.HBM)
    shapes = (
        jax.ShapeDtypeStruct((rows, dim), BF16),
        jax.ShapeDtypeStruct((1, width, codes), F32),
        jax.ShapeDtypeStruct((out_rows, dim), F32),
    )
    parts = pl.pallas_call(
        functools.partial(kernel, dp, subs),
        out_shape=shapes,
        in_specs=[hbm] * 3,
        out_specs=(vmem,) * 3,
        scratch_shapes=[
            pltpu.VMEM((subs, rows, dim), BF16),
            pltpu.VMEM((width, dim), BF16),
            pltpu.VMEM((width, codes), F32),
            pltpu.VMEM((codes, width + 16), BF16),
            pltpu.VMEM((subs, width, rows), BF16),
            pltpu.VMEM((subs, width, rows), BF16),
            pltpu.VMEM((2, width // 2, codes), BF16),
            pltpu.VMEM((dp, tile, LANES), BF16),
            pltpu.VMEM((width // 2, codes), BF16),
            pltpu.VMEM((width // 2, codes), BF16),
            pltpu.VMEM((dp // 2, width // 2, codes), BF16),
            pltpu.VMEM((dp - 1, tile, LANES), BF16),
            pltpu.VMEM((1, codes), F32),
            pltpu.VMEM((dp, 1, codes), F32),
            pltpu.VMEM((2, width // 2, codes), F32),
            pltpu.VMEM((subs, out_rows, LANES), F32),
            pltpu.VMEM((subs, out_rows, LANES), F32),
            dma((3,)),
            dma((subs,)),
            dma((subs,)),
            dma((7,)),
            dma((7,)),
        ],
        compiler_params=pltpu.CompilerParams(
            collective_id=0, has_side_effects=True, vmem_limit_bytes=40 * 1024 * 1024
        ),
    )(
        *(
            pltpu.with_memory_space_constraint(x, pltpu.HBM)
            for x in (samples, rotation.T, codebook.swapaxes(1, 2))
        )
    )
    recon, new_codes, cross = pl.pallas_call(
        write_kernel,
        out_shape=shapes,
        in_specs=[vmem] * 3,
        out_specs=(hbm,) * 3,
        scratch_shapes=[dma((3,))],
        compiler_params=pltpu.CompilerParams(vmem_limit_bytes=4 * 1024 * 1024),
    )(*parts)
    return recon, new_codes.swapaxes(1, 2), cross


def solution(mesh):
    in_specs = (P(("dp", "sub"), None), P(None, "sub"), P("sub", None, None))
    out_specs = (P(("dp", "sub"), None), P("sub", None, None), P(("dp", "sub"), None))
    return jax.shard_map(
        functools.partial(per_device, mesh.shape["dp"], mesh.shape["sub"]),
        mesh=mesh,
        in_specs=in_specs,
        out_specs=out_specs,
        check_vma=False,
    )
```

```python
import functools

import jax
import jax.numpy as jnp
from jax import lax
from jax.experimental import pallas as pl
from jax.experimental.pallas import tpu as pltpu
from jax.sharding import PartitionSpec as P

MESH = pl.DeviceIdType.MESH
F32 = jnp.float32
BF16 = jnp.bfloat16
LANES = 128
NT = (((1,), (1,)), ((), ()))
TN = (((0,), (0,)), ((), ()))


def peers(subs):
    half = subs // 2
    my_sub = lax.axis_index("sub")
    my_part = my_sub // half
    my_place = my_sub - my_part * half

    def wrap(index, count):
        return jnp.where(index >= count, index - count, index)

    steps = [(p, q) for p in range(2) for q in range(half)]

    def towards(k):
        p, q = steps[k]
        return wrap(my_part + p, 2) * half + wrap(my_place + q, half)

    def origin(k):
        p, q = steps[k]
        return wrap(my_part + 2 - p, 2) * half + wrap(my_place + half - q, half)

    return wrap, towards, origin


def remote(src, dst, send, recv, device):
    return pltpu.make_async_remote_copy(
        src_ref=src,
        dst_ref=dst,
        send_sem=send,
        recv_sem=recv,
        device_id=device,
        device_id_type=MESH,
    )


def gather_kernel(subs, samples_hbm, blocks, local_sem, block_send, block_recv):
    my_dp = lax.axis_index("dp")
    _, towards, _ = peers(subs)
    barrier = pltpu.get_barrier_semaphore()
    for k in range(1, subs):
        pl.semaphore_signal(barrier, inc=1, device_id=(my_dp, towards(k)), device_id_type=MESH)
    load = pltpu.make_async_copy(samples_hbm, blocks.at[0], local_sem)
    load.start()
    load.wait()
    pl.semaphore_wait(barrier, subs - 1)
    copies = [
        remote(
            blocks.at[0], blocks.at[k], block_send.at[k], block_recv.at[k], (my_dp, towards(k))
        )
        for k in range(subs - 1, 0, -1)
    ]
    for copy in copies:
        copy.start()
    for copy in copies:
        copy.wait()


def kernel(
    dp,
    subs,
    blocks,
    rotation_hbm,
    codebook_hbm,
    recon_ref,
    new_ref,
    cross_ref,
    rotation,
    code_own,
    code_tall,
    rec_out,
    rec_in,
    pack_s,
    pack_x,
    two_s,
    two_x,
    count_out,
    count_in,
    own_total,
    totals,
    cross_out,
    cross_in,
    local_sem,
    many_send,
    many_recv,
):
    my_dp = lax.axis_index("dp")
    my_sub = lax.axis_index("sub")
    wrap, towards, origin = peers(subs)
    _, rows, dim = blocks.shape
    width, codes = code_own.shape
    chunk = width // dp
    out_rows = cross_ref.shape[0]

    def along(t):
        return wrap(my_dp + t, dp)

    barrier = pltpu.get_barrier_semaphore()
    for k in range(1, subs):
        pl.semaphore_signal(barrier, inc=1, device_id=(my_dp, towards(k)), device_id_type=MESH)
    for t in range(1, dp):
        pl.semaphore_signal(barrier, inc=1, device_id=(along(t), my_sub), device_id_type=MESH)

    load_codes = pltpu.make_async_copy(codebook_hbm.at[0], code_own, local_sem.at[1])
    load_rotation = pltpu.make_async_copy(rotation_hbm, rotation, local_sem.at[2])
    load_codes.start()
    load_rotation.start()

    load_codes.wait()
    code_t = code_own[...]
    square = -0.5 * jnp.sum(code_t * code_t, axis=0, keepdims=True)
    high = square.astype(BF16).astype(F32)
    middle = (square - high).astype(BF16).astype(F32)
    low = square - high - middle
    row = lax.broadcasted_iota(jnp.int32, (16, codes), 0)
    split = jnp.where(row == 0, high, jnp.where(row == 1, middle, jnp.where(row == 2, low, 0.0)))
    code_tall[...] = jnp.concatenate([code_t, split], axis=0).T.astype(BF16)
    code_low = code_t.astype(BF16)
    load_rotation.wait()

    def assign(first, count):
        block = blocks[first : first + count].reshape(count * rows, dim)
        rotated = lax.dot_general(rotation[...], block, NT, preferred_element_type=F32).astype(BF16)
        wide = rotated.astype(F32)
        row_square = jnp.sum(wide * wide, axis=0, keepdims=True)
        tall = jnp.concatenate([rotated, jnp.ones((16, count * rows), BF16)], axis=0)
        inner = jnp.dot(code_tall[...], tall, preferred_element_type=F32)
        logits = -0.125 * (row_square - 2.0 * inner)
        powers = jnp.exp(logits - jnp.max(logits, axis=0, keepdims=True))
        weights = (powers * (1.0 / jnp.sum(powers, axis=0, keepdims=True))).astype(BF16)
        return weights, lax.dot_general(tall, weights, NT, preferred_element_type=F32), block

    def rebuild(first, count, weights, block):
        recon = jnp.dot(code_low, weights, preferred_element_type=F32).astype(BF16)
        for k in range(first, first + count):
            piece = recon[:, (k - first) * rows : (k - first + 1) * rows]
            if k == 0:
                rec_in[my_sub] = piece
            else:
                rec_out[k] = piece
        return jnp.dot(recon, block, preferred_element_type=F32)

    groups = [(k, 2) for k in range(0, subs, 2)]
    sums = jnp.zeros((width + 16, codes), F32)
    cross = jnp.zeros((width, dim), F32)
    for first, count in groups[:-1]:
        weights, part, block = assign(first, count)
        sums += part
        cross += rebuild(first, count, weights, block)
    weights, part, block = assign(*groups[-1])
    sums += part

    pieces = sums[:width].reshape(dp, chunk, codes)
    pieces = jnp.concatenate([pieces[..., j : j + LANES] for j in range(0, codes, LANES)], axis=1)
    fill = pack_s.shape[1] - pieces.shape[1]
    if fill:
        pieces = jnp.concatenate([pieces, jnp.zeros((dp, fill, LANES), F32)], axis=1)
    pack_s[...] = pieces.astype(BF16)

    def spread(pack, two, t, s):
        return remote(
            pack.at[along(t)], two.at[t - 1], many_send.at[s], many_recv.at[s], (along(t), my_sub)
        )

    pl.semaphore_wait(barrier, subs + dp - 2)
    for t in range(1, dp):
        spread(pack_s, two_s, t, 0).start()

    cross += rebuild(*groups[-1], weights, block)
    tile = pack_x.shape[1]
    pieces = cross.T.reshape(dp, 2, tile, width)
    pack_x[...] = jnp.concatenate([pieces[:, 0], pieces[:, 1]], axis=2).astype(BF16)
    for t in range(1, dp):
        spread(pack_x, two_x, t, 1).start()

    count_out[...] = sums[width : width + 1]

    def send_count(t):
        return remote(
            count_out, count_in.at[my_dp], many_send.at[2], many_recv.at[2], (along(t), my_sub)
        )

    for t in range(1, dp):
        send_count(t).start()
    count_in[my_dp] = count_out[...]

    def send_recon(k):
        device = (my_dp, origin(k))
        return remote(rec_out.at[k], rec_in.at[my_sub], many_send.at[3], many_recv.at[3], device)

    for k in range(1, subs):
        send_recon(k).start()

    def bulk(buffer, count, s):
        part = buffer.at[pl.ds(0, count)]
        return remote(part, part, many_send.at[s], many_recv.at[s], (along(1), my_sub))

    bulk(two_s, dp - 1, 0).wait_recv()
    total = pack_s[my_dp].astype(F32) + jnp.sum(two_s[...].astype(F32), axis=0)
    own_total[...] = total.astype(BF16)

    def share(t):
        return remote(
            own_total, totals.at[my_dp], many_send.at[4], many_recv.at[4], (along(t), my_sub)
        )

    for t in range(1, dp):
        share(t).start()
    totals[my_dp] = own_total[...]

    bulk(two_x, dp - 1, 1).wait_recv()
    total_x = pack_x[my_dp].astype(F32) + jnp.sum(two_x[...].astype(F32), axis=0)
    total_x = jnp.concatenate([total_x[:, :width], total_x[:, width : 2 * width]], axis=0)
    cross_out[...] = jnp.concatenate([total_x, total_x], axis=1).reshape(cross_out.shape)

    def send_cross(k):
        peer = towards(k)
        return remote(
            cross_out.at[peer], cross_in.at[my_sub], many_send.at[5], many_recv.at[5], (my_dp, peer)
        )

    for k in range(1, subs):
        send_cross(k).start()
    cross_in[my_sub] = cross_out[my_sub]

    bulk(rec_in, subs - 1, 3).wait_recv()
    recon_ref[...] = rec_in[...].reshape(dim, rows).astype(F32).T.astype(BF16)

    bulk(count_in, dp - 1, 2).wait_recv()
    counts = 1.0 + jnp.sum(count_in[...], axis=0)
    bulk(totals, dp - 1, 4).wait_recv()
    all_totals = totals[...].astype(F32)
    for j in range(codes // LANES):
        lanes = slice(j * LANES, (j + 1) * LANES)
        part = all_totals[:, j * chunk : (j + 1) * chunk].reshape(width, LANES)
        new_ref[0, :, lanes] = (part + code_own[:, lanes]) / counts[:, lanes]

    bulk(cross_in, subs - 1, 5).wait_recv()
    cross_ref[...] = jnp.concatenate([cross_in[s][:, :width] for s in range(subs)], axis=1)

    bulk(two_s, dp - 1, 0).wait_send()
    bulk(two_x, dp - 1, 1).wait_send()
    bulk(count_in, dp - 1, 2).wait_send()
    bulk(rec_in, subs - 1, 3).wait_send()
    bulk(totals, dp - 1, 4).wait_send()
    bulk(cross_in, subs - 1, 5).wait_send()


def write_kernel(recon_ref, new_ref, cross_ref, recon_out, new_out, cross_out, sems):
    pairs = ((recon_ref, recon_out), (new_ref, new_out), (cross_ref, cross_out))
    copies = [pltpu.make_async_copy(s, d, sems.at[i]) for i, (s, d) in enumerate(pairs)]
    for copy in copies:
        copy.start()
    for copy in copies:
        copy.wait()


def per_device(dp, subs, samples, rotation, codebook):
    rows, dim = samples.shape
    codes, width = codebook.shape[1:]
    chunk = max(16, width * codes // (dp * LANES))
    out_rows = dim // (dp * subs)
    tile = dim // dp // 2
    dma = pltpu.SemaphoreType.DMA
    vmem = pl.BlockSpec(memory_space=pltpu.VMEM)
    hbm = pl.BlockSpec(memory_space=pltpu.HBM)
    shapes = (
        jax.ShapeDtypeStruct((rows, dim), BF16),
        jax.ShapeDtypeStruct((1, width, codes), F32),
        jax.ShapeDtypeStruct((out_rows, dim), F32),
    )
    blocks = pl.pallas_call(
        functools.partial(gather_kernel, subs),
        out_shape=jax.ShapeDtypeStruct((subs, rows, dim), BF16),
        in_specs=[hbm],
        out_specs=vmem,
        scratch_shapes=[dma, dma((subs,)), dma((subs,))],
        compiler_params=pltpu.CompilerParams(
            collective_id=0, has_side_effects=True, vmem_limit_bytes=16 * 1024 * 1024
        ),
    )(pltpu.with_memory_space_constraint(samples, pltpu.HBM))
    parts = pl.pallas_call(
        functools.partial(kernel, dp, subs),
        out_shape=shapes,
        in_specs=[vmem, hbm, hbm],
        out_specs=(vmem,) * 3,
        scratch_shapes=[
            pltpu.VMEM((width, dim), BF16),
            pltpu.VMEM((width, codes), F32),
            pltpu.VMEM((codes, width + 16), BF16),
            pltpu.VMEM((subs, width, rows), BF16),
            pltpu.VMEM((subs, width, rows), BF16),
            pltpu.VMEM((dp, chunk, LANES), BF16),
            pltpu.VMEM((dp, tile, LANES), BF16),
            pltpu.VMEM((dp - 1, chunk, LANES), BF16),
            pltpu.VMEM((dp - 1, tile, LANES), BF16),
            pltpu.VMEM((1, codes), F32),
            pltpu.VMEM((dp, 1, codes), F32),
            pltpu.VMEM((chunk, LANES), BF16),
            pltpu.VMEM((dp, chunk, LANES), BF16),
            pltpu.VMEM((subs, out_rows, LANES), F32),
            pltpu.VMEM((subs, out_rows, LANES), F32),
            dma((3,)),
            dma((6,)),
            dma((6,)),
        ],
        compiler_params=pltpu.CompilerParams(
            collective_id=1, has_side_effects=True, vmem_limit_bytes=40 * 1024 * 1024
        ),
    )(
        blocks,
        pltpu.with_memory_space_constraint(rotation.T, pltpu.HBM),
        pltpu.with_memory_space_constraint(codebook.swapaxes(1, 2), pltpu.HBM),
    )
    recon, new_codes, cross = pl.pallas_call(
        write_kernel,
        out_shape=shapes,
        in_specs=[vmem] * 3,
        out_specs=(hbm,) * 3,
        scratch_shapes=[dma((3,))],
        compiler_params=pltpu.CompilerParams(vmem_limit_bytes=4 * 1024 * 1024),
    )(*parts)
    return recon, new_codes.swapaxes(1, 2), cross


def solution(mesh):
    in_specs = (P(("dp", "sub"), None), P(None, "sub"), P("sub", None, None))
    out_specs = (P(("dp", "sub"), None), P("sub", None, None), P(("dp", "sub"), None))
    return jax.shard_map(
        functools.partial(per_device, mesh.shape["dp"], mesh.shape["sub"]),
        mesh=mesh,
        in_specs=in_specs,
        out_specs=out_specs,
        check_vma=False,
    )
```

```python
import functools

import jax
import jax.numpy as jnp
from jax import lax
from jax.experimental import pallas as pl
from jax.experimental.pallas import tpu as pltpu
from jax.sharding import PartitionSpec as P

MESH = pl.DeviceIdType.MESH
F32 = jnp.float32
BF16 = jnp.bfloat16
LANES = 128
NT = (((1,), (1,)), ((), ()))
TN = (((0,), (0,)), ((), ()))


def peers(subs):
    half = subs // 2
    my_sub = lax.axis_index("sub")
    my_part = my_sub // half
    my_place = my_sub - my_part * half

    def wrap(index, count):
        return jnp.where(index >= count, index - count, index)

    steps = [(p, q) for p in range(2) for q in range(half)]

    def towards(k):
        p, q = steps[k]
        return wrap(my_part + p, 2) * half + wrap(my_place + q, half)

    def origin(k):
        p, q = steps[k]
        return wrap(my_part + 2 - p, 2) * half + wrap(my_place + half - q, half)

    return wrap, towards, origin


def remote(src, dst, send, recv, device):
    return pltpu.make_async_remote_copy(
        src_ref=src,
        dst_ref=dst,
        send_sem=send,
        recv_sem=recv,
        device_id=device,
        device_id_type=MESH,
    )


def lengthen(code_t):
    codes = code_t.shape[1]
    square = -0.5 * jnp.sum(code_t * code_t, axis=0, keepdims=True)
    high = square.astype(BF16).astype(F32)
    middle = (square - high).astype(BF16).astype(F32)
    low = square - high - middle
    row = lax.broadcasted_iota(jnp.int32, (16, codes), 0)
    split = jnp.where(row == 0, high, jnp.where(row == 1, middle, jnp.where(row == 2, low, 0.0)))
    return jnp.concatenate([code_t, split], axis=0).T.astype(BF16)


def assign(rotation, code_tall, block):
    rotated = lax.dot_general(rotation, block, NT, preferred_element_type=F32).astype(BF16)
    wide = rotated.astype(F32)
    row_square = jnp.sum(wide * wide, axis=0, keepdims=True)
    tall = jnp.concatenate([rotated, jnp.ones((16, block.shape[0]), BF16)], axis=0)
    inner = jnp.dot(code_tall, tall, preferred_element_type=F32)
    logits = -0.125 * (row_square - 2.0 * inner)
    powers = jnp.exp(logits - jnp.max(logits, axis=0, keepdims=True))
    weights = (powers * (1.0 / jnp.sum(powers, axis=0, keepdims=True))).astype(BF16)
    return weights, lax.dot_general(tall, weights, NT, preferred_element_type=F32)


def gather_kernel(
    subs,
    samples_hbm,
    rotation_hbm,
    codebook_hbm,
    blocks,
    rotation,
    code_own,
    code_tall,
    rec,
    sums_ref,
    cross_ref,
    local_sem,
    block_send,
    block_recv,
):
    my_dp = lax.axis_index("dp")
    _, towards, _ = peers(subs)
    barrier = pltpu.get_barrier_semaphore()
    for k in range(1, subs):
        pl.semaphore_signal(barrier, inc=1, device_id=(my_dp, towards(k)), device_id_type=MESH)
    load_samples = pltpu.make_async_copy(samples_hbm, blocks.at[0], local_sem.at[0])
    load_codes = pltpu.make_async_copy(codebook_hbm.at[0], code_own, local_sem.at[1])
    load_rotation = pltpu.make_async_copy(rotation_hbm, rotation, local_sem.at[2])
    load_samples.start()
    load_codes.start()
    load_rotation.start()
    load_samples.wait()
    pl.semaphore_wait(barrier, subs - 1)
    copies = [
        remote(
            blocks.at[0], blocks.at[k], block_send.at[k], block_recv.at[k], (my_dp, towards(k))
        )
        for k in range(1, subs)
    ]
    for copy in copies:
        copy.start()
    load_codes.wait()
    load_rotation.wait()
    code_tall[...] = lengthen(code_own[...])
    code_low = code_own[...].astype(BF16)
    for k in range(subs // 2):
        if k > 0:
            copies[k - 1].wait_recv()
        weights, part = assign(rotation[...], code_tall[...], blocks[k])
        recon = jnp.dot(code_low, weights, preferred_element_type=F32).astype(BF16)
        rec[k] = recon
        whole = jnp.dot(recon, blocks[k], preferred_element_type=F32)
        if k == 0:
            sums_ref[...] = part
            cross_ref[...] = whole
        else:
            sums_ref[...] += part
            cross_ref[...] += whole
    for copy in copies[subs // 2 - 1 :]:
        copy.wait_recv()
    for copy in copies:
        copy.wait_send()


def kernel(
    dp,
    subs,
    blocks,
    rotation,
    code_own,
    code_tall,
    rec_first,
    sums_first,
    cross_first,
    recon_ref,
    new_ref,
    cross_ref,
    rec_out,
    rec_in,
    pack_s,
    pack_x,
    two_s,
    two_x,
    count_out,
    count_in,
    own_total,
    totals,
    cross_out,
    cross_in,
    many_send,
    many_recv,
):
    my_dp = lax.axis_index("dp")
    my_sub = lax.axis_index("sub")
    wrap, towards, origin = peers(subs)
    _, rows, dim = blocks.shape
    width, codes = code_own.shape
    chunk = width // dp
    out_rows = cross_ref.shape[0]

    def along(t):
        return wrap(my_dp + t, dp)

    barrier = pltpu.get_barrier_semaphore()
    for k in range(1, subs):
        pl.semaphore_signal(barrier, inc=1, device_id=(my_dp, towards(k)), device_id_type=MESH)
    for t in range(1, dp):
        pl.semaphore_signal(barrier, inc=1, device_id=(along(t), my_sub), device_id_type=MESH)

    code_low = code_own[...].astype(BF16)

    def work(first, count):
        block = blocks[first : first + count].reshape(count * rows, dim)
        return *assign(rotation[...], code_tall[...], block), block

    def rebuild(first, count, weights, block):
        recon = jnp.dot(code_low, weights, preferred_element_type=F32).astype(BF16)
        for k in range(first, first + count):
            rec_out[k] = recon[:, (k - first) * rows : (k - first + 1) * rows]
        return jnp.dot(recon, block, preferred_element_type=F32)

    rec_in[my_sub] = rec_first[0]
    for k in range(1, subs // 2):
        rec_out[k] = rec_first[k]
    groups = [(k, 2) for k in range(subs // 2, subs, 2)]
    sums = sums_first[...]
    cross = cross_first[...]
    for first, count in groups[:-1]:
        weights, part, block = work(first, count)
        sums += part
        cross += rebuild(first, count, weights, block)
    weights, part, block = work(*groups[-1])
    sums += part

    pieces = sums[:width].reshape(dp, chunk, codes)
    pieces = jnp.concatenate([pieces[..., j : j + LANES] for j in range(0, codes, LANES)], axis=1)
    fill = pack_s.shape[1] - pieces.shape[1]
    if fill:
        pieces = jnp.concatenate([pieces, jnp.zeros((dp, fill, LANES), F32)], axis=1)
    pack_s[...] = pieces.astype(BF16)

    def spread(pack, two, t, s):
        return remote(
            pack.at[along(t)], two.at[t - 1], many_send.at[s], many_recv.at[s], (along(t), my_sub)
        )

    pl.semaphore_wait(barrier, subs + dp - 2)
    for t in range(1, dp):
        spread(pack_s, two_s, t, 0).start()

    cross += rebuild(*groups[-1], weights, block)
    tile = pack_x.shape[1]
    pieces = cross.T.reshape(dp, 2, tile, width)
    pack_x[...] = jnp.concatenate([pieces[:, 0], pieces[:, 1]], axis=2).astype(BF16)
    for t in range(1, dp):
        spread(pack_x, two_x, t, 1).start()

    count_out[...] = sums[width : width + 1]

    def send_count(t):
        return remote(
            count_out, count_in.at[my_dp], many_send.at[2], many_recv.at[2], (along(t), my_sub)
        )

    for t in range(1, dp):
        send_count(t).start()
    count_in[my_dp] = count_out[...]

    def send_recon(k):
        device = (my_dp, origin(k))
        return remote(rec_out.at[k], rec_in.at[my_sub], many_send.at[3], many_recv.at[3], device)

    for k in range(1, subs):
        send_recon(k).start()

    def bulk(buffer, count, s):
        part = buffer.at[pl.ds(0, count)]
        return remote(part, part, many_send.at[s], many_recv.at[s], (along(1), my_sub))

    bulk(two_s, dp - 1, 0).wait_recv()
    total = pack_s[my_dp].astype(F32) + jnp.sum(two_s[...].astype(F32), axis=0)
    own_total[...] = total.astype(BF16)

    def share(t):
        return remote(
            own_total, totals.at[my_dp], many_send.at[4], many_recv.at[4], (along(t), my_sub)
        )

    for t in range(1, dp):
        share(t).start()
    totals[my_dp] = own_total[...]

    bulk(two_x, dp - 1, 1).wait_recv()
    total_x = pack_x[my_dp].astype(F32) + jnp.sum(two_x[...].astype(F32), axis=0)
    total_x = jnp.concatenate([total_x[:, :width], total_x[:, width : 2 * width]], axis=0)
    cross_out[...] = jnp.concatenate([total_x, total_x], axis=1).reshape(cross_out.shape)

    def send_cross(k):
        peer = towards(k)
        return remote(
            cross_out.at[peer], cross_in.at[my_sub], many_send.at[5], many_recv.at[5], (my_dp, peer)
        )

    for k in range(1, subs):
        send_cross(k).start()
    cross_in[my_sub] = cross_out[my_sub]

    bulk(rec_in, subs - 1, 3).wait_recv()
    recon_ref[...] = rec_in[...].reshape(dim, rows).astype(F32).T.astype(BF16)

    bulk(count_in, dp - 1, 2).wait_recv()
    counts = 1.0 + jnp.sum(count_in[...], axis=0)
    bulk(totals, dp - 1, 4).wait_recv()
    all_totals = totals[...].astype(F32)
    for j in range(codes // LANES):
        lanes = slice(j * LANES, (j + 1) * LANES)
        part = all_totals[:, j * chunk : (j + 1) * chunk].reshape(width, LANES)
        new_ref[0, :, lanes] = (part + code_own[:, lanes]) / counts[:, lanes]

    bulk(cross_in, subs - 1, 5).wait_recv()
    cross_ref[...] = jnp.concatenate([cross_in[s][:, :width] for s in range(subs)], axis=1)

    bulk(two_s, dp - 1, 0).wait_send()
    bulk(two_x, dp - 1, 1).wait_send()
    bulk(count_in, dp - 1, 2).wait_send()
    bulk(rec_in, subs - 1, 3).wait_send()
    bulk(totals, dp - 1, 4).wait_send()
    bulk(cross_in, subs - 1, 5).wait_send()


def write_kernel(recon_ref, new_ref, cross_ref, recon_out, new_out, cross_out, sems):
    pairs = ((recon_ref, recon_out), (new_ref, new_out), (cross_ref, cross_out))
    copies = [pltpu.make_async_copy(s, d, sems.at[i]) for i, (s, d) in enumerate(pairs)]
    for copy in copies:
        copy.start()
    for copy in copies:
        copy.wait()


def per_device(dp, subs, samples, rotation, codebook):
    rows, dim = samples.shape
    codes, width = codebook.shape[1:]
    chunk = max(16, width * codes // (dp * LANES))
    out_rows = dim // (dp * subs)
    tile = dim // dp // 2
    dma = pltpu.SemaphoreType.DMA
    vmem = pl.BlockSpec(memory_space=pltpu.VMEM)
    hbm = pl.BlockSpec(memory_space=pltpu.HBM)
    shapes = (
        jax.ShapeDtypeStruct((rows, dim), BF16),
        jax.ShapeDtypeStruct((1, width, codes), F32),
        jax.ShapeDtypeStruct((out_rows, dim), F32),
    )
    first = pl.pallas_call(
        functools.partial(gather_kernel, subs),
        out_shape=(
            jax.ShapeDtypeStruct((subs, rows, dim), BF16),
            jax.ShapeDtypeStruct((width, dim), BF16),
            jax.ShapeDtypeStruct((width, codes), F32),
            jax.ShapeDtypeStruct((codes, width + 16), BF16),
            jax.ShapeDtypeStruct((subs // 2, width, rows), BF16),
            jax.ShapeDtypeStruct((width + 16, codes), F32),
            jax.ShapeDtypeStruct((width, dim), F32),
        ),
        in_specs=[hbm] * 3,
        out_specs=(vmem,) * 7,
        scratch_shapes=[dma((3,)), dma((subs,)), dma((subs,))],
        compiler_params=pltpu.CompilerParams(
            collective_id=0, has_side_effects=True, vmem_limit_bytes=40 * 1024 * 1024
        ),
    )(
        *(
            pltpu.with_memory_space_constraint(x, pltpu.HBM)
            for x in (samples, rotation.T, codebook.swapaxes(1, 2))
        )
    )
    parts = pl.pallas_call(
        functools.partial(kernel, dp, subs),
        out_shape=shapes,
        in_specs=[vmem] * 7,
        out_specs=(vmem,) * 3,
        scratch_shapes=[
            pltpu.VMEM((subs, width, rows), BF16),
            pltpu.VMEM((subs, width, rows), BF16),
            pltpu.VMEM((dp, chunk, LANES), BF16),
            pltpu.VMEM((dp, tile, LANES), BF16),
            pltpu.VMEM((dp - 1, chunk, LANES), BF16),
            pltpu.VMEM((dp - 1, tile, LANES), BF16),
            pltpu.VMEM((1, codes), F32),
            pltpu.VMEM((dp, 1, codes), F32),
            pltpu.VMEM((chunk, LANES), BF16),
            pltpu.VMEM((dp, chunk, LANES), BF16),
            pltpu.VMEM((subs, out_rows, LANES), F32),
            pltpu.VMEM((subs, out_rows, LANES), F32),
            dma((6,)),
            dma((6,)),
        ],
        compiler_params=pltpu.CompilerParams(
            collective_id=1, has_side_effects=True, vmem_limit_bytes=40 * 1024 * 1024
        ),
    )(*first)
    recon, new_codes, cross = pl.pallas_call(
        write_kernel,
        out_shape=shapes,
        in_specs=[vmem] * 3,
        out_specs=(hbm,) * 3,
        scratch_shapes=[dma((3,))],
        compiler_params=pltpu.CompilerParams(vmem_limit_bytes=4 * 1024 * 1024),
    )(*parts)
    return recon, new_codes.swapaxes(1, 2), cross


def solution(mesh):
    in_specs = (P(("dp", "sub"), None), P(None, "sub"), P("sub", None, None))
    out_specs = (P(("dp", "sub"), None), P("sub", None, None), P(("dp", "sub"), None))
    return jax.shard_map(
        functools.partial(per_device, mesh.shape["dp"], mesh.shape["sub"]),
        mesh=mesh,
        in_specs=in_specs,
        out_specs=out_specs,
        check_vma=False,
    )
```

```python
import functools

import jax
import jax.numpy as jnp
from jax import lax
from jax.experimental import pallas as pl
from jax.experimental.pallas import tpu as pltpu
from jax.sharding import PartitionSpec as P

MESH = pl.DeviceIdType.MESH
F32 = jnp.float32
BF16 = jnp.bfloat16
LANES = 128
NT = (((1,), (1,)), ((), ()))
TN = (((0,), (0,)), ((), ()))


def kernel(
    dp,
    subs,
    samples_hbm,
    rotation_hbm,
    codebook_hbm,
    recon_ref,
    new_ref,
    cross_ref,
    blocks,
    rotation,
    code_own,
    code_tall,
    rec_out,
    rec_in,
    pack_s,
    pack_x,
    two_s,
    two_x,
    count_out,
    count_in,
    own_total,
    totals,
    cross_out,
    cross_in,
    local_sem,
    block_send,
    block_recv,
    many_send,
    many_recv,
):
    half = subs // 2
    my_dp = lax.axis_index("dp")
    my_sub = lax.axis_index("sub")
    my_part = my_sub // half
    my_place = my_sub - my_part * half
    _, rows, dim = blocks.shape
    width, codes = code_own.shape
    chunk = width // dp
    out_rows = cross_ref.shape[0]

    def wrap(index, count):
        return jnp.where(index >= count, index - count, index)

    steps = [(p, q) for p in range(2) for q in range(half)]

    def towards(k):
        p, q = steps[k]
        return wrap(my_part + p, 2) * half + wrap(my_place + q, half)

    def origin(k):
        p, q = steps[k]
        return wrap(my_part + 2 - p, 2) * half + wrap(my_place + half - q, half)

    def along(t):
        return wrap(my_dp + t, dp)

    barrier = pltpu.get_barrier_semaphore()
    for t in range(1, dp):
        pl.semaphore_signal(barrier, inc=1, device_id=(along(t), my_sub), device_id_type=MESH)
    for k in range(1, subs):
        pl.semaphore_signal(barrier, inc=1, device_id=(my_dp, towards(k)), device_id_type=MESH)

    load_samples = pltpu.make_async_copy(samples_hbm, blocks.at[0], local_sem.at[0])
    load_codes = pltpu.make_async_copy(codebook_hbm.at[0], code_own, local_sem.at[1])
    load_rotation = pltpu.make_async_copy(rotation_hbm, rotation, local_sem.at[2])
    load_codes.start()
    load_samples.start()
    load_rotation.start()

    def remote(src, dst, send, recv, device):
        return pltpu.make_async_remote_copy(
            src_ref=src,
            dst_ref=dst,
            send_sem=send,
            recv_sem=recv,
            device_id=device,
            device_id_type=MESH,
        )

    def block_copy(k):
        return remote(
            blocks.at[0], blocks.at[k], block_send.at[k], block_recv.at[k], (my_dp, towards(k))
        )

    load_samples.wait()
    pl.semaphore_wait(barrier, subs + dp - 2)
    for k in range(subs - 1, 0, -1):
        block_copy(k).start()

    load_codes.wait()
    code_t = code_own[...]
    square = -0.5 * jnp.sum(code_t * code_t, axis=0, keepdims=True)
    high = square.astype(BF16).astype(F32)
    middle = (square - high).astype(BF16).astype(F32)
    low = square - high - middle
    row = lax.broadcasted_iota(jnp.int32, (16, codes), 0)
    split = jnp.where(row == 0, high, jnp.where(row == 1, middle, jnp.where(row == 2, low, 0.0)))
    code_tall[...] = jnp.concatenate([code_t, split], axis=0).T.astype(BF16)
    code_low = code_t.astype(BF16)
    load_rotation.wait()

    def assign(first, count):
        for k in range(max(first, 1), first + count):
            block_copy(k).wait_recv()
        block = blocks[first : first + count].reshape(count * rows, dim)
        rotated = lax.dot_general(rotation[...], block, NT, preferred_element_type=F32).astype(BF16)
        wide = rotated.astype(F32)
        row_square = jnp.sum(wide * wide, axis=0, keepdims=True)
        tall = jnp.concatenate([rotated, jnp.ones((16, count * rows), BF16)], axis=0)
        inner = jnp.dot(code_tall[...], tall, preferred_element_type=F32)
        logits = -0.125 * (row_square - 2.0 * inner)
        powers = jnp.exp(logits - jnp.max(logits, axis=0, keepdims=True))
        weights = (powers * (1.0 / jnp.sum(powers, axis=0, keepdims=True))).astype(BF16)
        return weights, lax.dot_general(tall, weights, NT, preferred_element_type=F32), block

    def rebuild(first, count, weights, block):
        recon = jnp.dot(code_low, weights, preferred_element_type=F32).astype(BF16)
        for k in range(first, first + count):
            piece = recon[:, (k - first) * rows : (k - first + 1) * rows]
            if k == 0:
                rec_in[my_sub] = piece
            else:
                rec_out[k] = piece
        return jnp.dot(recon, block, preferred_element_type=F32)

    groups = [(0, 1), (1, 1)] + [(k, 2) for k in range(2, subs, 2)]
    sums = jnp.zeros((width + 16, codes), F32)
    cross = jnp.zeros((width, dim), F32)
    for first, count in groups[:-1]:
        weights, part, block = assign(first, count)
        sums += part
        cross += rebuild(first, count, weights, block)
    weights, part, block = assign(*groups[-1])
    sums += part

    pieces = sums[:width].reshape(dp, chunk, codes)
    pieces = jnp.concatenate([pieces[..., j : j + LANES] for j in range(0, codes, LANES)], axis=1)
    fill = pack_s.shape[1] - pieces.shape[1]
    if fill:
        pieces = jnp.concatenate([pieces, jnp.zeros((dp, fill, LANES), F32)], axis=1)
    pack_s[...] = pieces.astype(BF16)

    def spread(pack, two, t, s):
        return remote(
            pack.at[along(t)], two.at[t - 1], many_send.at[s], many_recv.at[s], (along(t), my_sub)
        )

    for t in range(1, dp):
        spread(pack_s, two_s, t, 0).start()

    cross += rebuild(*groups[-1], weights, block)
    tile = pack_x.shape[1]
    pieces = cross.T.reshape(dp, 2, tile, width)
    pack_x[...] = jnp.concatenate([pieces[:, 0], pieces[:, 1]], axis=2).astype(BF16)
    for t in range(1, dp):
        spread(pack_x, two_x, t, 1).start()

    count_out[...] = sums[width : width + 1]

    def send_count(t):
        return remote(
            count_out, count_in.at[my_dp], many_send.at[2], many_recv.at[2], (along(t), my_sub)
        )

    for t in range(1, dp):
        send_count(t).start()
    count_in[my_dp] = count_out[...]

    def send_recon(k):
        device = (my_dp, origin(k))
        return remote(rec_out.at[k], rec_in.at[my_sub], many_send.at[3], many_recv.at[3], device)

    for k in range(1, subs):
        send_recon(k).start()

    def bulk(buffer, count, s):
        part = buffer.at[pl.ds(0, count)]
        return remote(part, part, many_send.at[s], many_recv.at[s], (along(1), my_sub))

    bulk(two_s, dp - 1, 0).wait_recv()
    total = pack_s[my_dp].astype(F32) + jnp.sum(two_s[...].astype(F32), axis=0)
    own_total[...] = total.astype(BF16)

    def share(t):
        return remote(
            own_total, totals.at[my_dp], many_send.at[4], many_recv.at[4], (along(t), my_sub)
        )

    for t in range(1, dp):
        share(t).start()
    totals[my_dp] = own_total[...]

    bulk(two_x, dp - 1, 1).wait_recv()
    total_x = pack_x[my_dp].astype(F32) + jnp.sum(two_x[...].astype(F32), axis=0)
    total_x = jnp.concatenate([total_x[:, :width], total_x[:, width : 2 * width]], axis=0)
    cross_out[...] = jnp.concatenate([total_x, total_x], axis=1).reshape(cross_out.shape)

    def send_cross(k):
        peer = towards(k)
        return remote(
            cross_out.at[peer], cross_in.at[my_sub], many_send.at[5], many_recv.at[5], (my_dp, peer)
        )

    for k in range(1, subs):
        send_cross(k).start()
    cross_in[my_sub] = cross_out[my_sub]

    bulk(rec_in, subs - 1, 3).wait_recv()
    recon_ref[...] = rec_in[...].reshape(dim, rows).astype(F32).T.astype(BF16)

    bulk(count_in, dp - 1, 2).wait_recv()
    counts = 1.0 + jnp.sum(count_in[...], axis=0)
    bulk(totals, dp - 1, 4).wait_recv()
    all_totals = totals[...].astype(F32)
    for j in range(codes // LANES):
        lanes = slice(j * LANES, (j + 1) * LANES)
        part = all_totals[:, j * chunk : (j + 1) * chunk].reshape(width, LANES)
        new_ref[0, :, lanes] = (part + code_own[:, lanes]) / counts[:, lanes]

    bulk(cross_in, subs - 1, 5).wait_recv()
    cross_ref[...] = jnp.concatenate([cross_in[s][:, :width] for s in range(subs)], axis=1)

    for k in range(1, subs):
        block_copy(k).wait_send()
    bulk(two_s, dp - 1, 0).wait_send()
    bulk(two_x, dp - 1, 1).wait_send()
    bulk(count_in, dp - 1, 2).wait_send()
    bulk(rec_in, subs - 1, 3).wait_send()
    bulk(totals, dp - 1, 4).wait_send()
    bulk(cross_in, subs - 1, 5).wait_send()


def write_kernel(recon_ref, new_ref, cross_ref, recon_out, new_out, cross_out, sems):
    pairs = ((recon_ref, recon_out), (new_ref, new_out), (cross_ref, cross_out))
    copies = [pltpu.make_async_copy(s, d, sems.at[i]) for i, (s, d) in enumerate(pairs)]
    for copy in copies:
        copy.start()
    for copy in copies:
        copy.wait()


def per_device(dp, subs, samples, rotation, codebook):
    rows, dim = samples.shape
    codes, width = codebook.shape[1:]
    chunk = max(16, width * codes // (dp * LANES))
    out_rows = dim // (dp * subs)
    tile = dim // dp // 2
    dma = pltpu.SemaphoreType.DMA
    vmem = pl.BlockSpec(memory_space=pltpu.VMEM)
    hbm = pl.BlockSpec(memory_space=pltpu.HBM)
    shapes = (
        jax.ShapeDtypeStruct((rows, dim), BF16),
        jax.ShapeDtypeStruct((1, width, codes), F32),
        jax.ShapeDtypeStruct((out_rows, dim), F32),
    )
    parts = pl.pallas_call(
        functools.partial(kernel, dp, subs),
        out_shape=shapes,
        in_specs=[hbm] * 3,
        out_specs=(vmem,) * 3,
        scratch_shapes=[
            pltpu.VMEM((subs, rows, dim), BF16),
            pltpu.VMEM((width, dim), BF16),
            pltpu.VMEM((width, codes), F32),
            pltpu.VMEM((codes, width + 16), BF16),
            pltpu.VMEM((subs, width, rows), BF16),
            pltpu.VMEM((subs, width, rows), BF16),
            pltpu.VMEM((dp, chunk, LANES), BF16),
            pltpu.VMEM((dp, tile, LANES), BF16),
            pltpu.VMEM((dp - 1, chunk, LANES), BF16),
            pltpu.VMEM((dp - 1, tile, LANES), BF16),
            pltpu.VMEM((1, codes), F32),
            pltpu.VMEM((dp, 1, codes), F32),
            pltpu.VMEM((chunk, LANES), BF16),
            pltpu.VMEM((dp, chunk, LANES), BF16),
            pltpu.VMEM((subs, out_rows, LANES), F32),
            pltpu.VMEM((subs, out_rows, LANES), F32),
            dma((3,)),
            dma((subs,)),
            dma((subs,)),
            dma((6,)),
            dma((6,)),
        ],
        compiler_params=pltpu.CompilerParams(
            collective_id=0, has_side_effects=True, vmem_limit_bytes=40 * 1024 * 1024
        ),
    )(
        *(
            pltpu.with_memory_space_constraint(x, pltpu.HBM)
            for x in (samples, rotation.T, codebook.swapaxes(1, 2))
        )
    )
    recon, new_codes, cross = pl.pallas_call(
        write_kernel,
        out_shape=shapes,
        in_specs=[vmem] * 3,
        out_specs=(hbm,) * 3,
        scratch_shapes=[dma((3,))],
        compiler_params=pltpu.CompilerParams(vmem_limit_bytes=4 * 1024 * 1024),
    )(*parts)
    return recon, new_codes.swapaxes(1, 2), cross


def solution(mesh):
    in_specs = (P(("dp", "sub"), None), P(None, "sub"), P("sub", None, None))
    out_specs = (P(("dp", "sub"), None), P("sub", None, None), P(("dp", "sub"), None))
    return jax.shard_map(
        functools.partial(per_device, mesh.shape["dp"], mesh.shape["sub"]),
        mesh=mesh,
        in_specs=in_specs,
        out_specs=out_specs,
        check_vma=False,
    )
```
